256 devices in a mesh: leaf: 64 (over y, z, core), rhs: 4 (over x).
Axes of the slice: x: 4, y: 4, z: 8, core: 2. Of those that a mesh axis runs over, the one named last changes fastest.
Arguments:
- rhs_cols: bfloat16 [64, 524288], P('rhs', 'leaf'), may hold values from -6 to 6
- near_blocks: bfloat16 [4096, 4, 128, 128], P('leaf'), may hold values from -0.25 to 0.25
- near_list: int32 [4096, 4], P('leaf'), may hold values from 0 to 4095, as said below
- leaf_basis: bfloat16 [4096, 32, 128], P('leaf'), may hold values from -0.5 to 0.5
- inner_transfer: bfloat16 [8128, 32, 32], P('leaf'), may hold values from -0.75 to 0.75
- inner_coupling: bfloat16 [8128, 6, 32, 32], P('leaf'), as said below
- inner_far: int32 [8128, 6], P('leaf'), may hold values from 0 to 4095, as said below
- top_transfer: bfloat16 [62, 32, 32], replicated, may hold values from -0.75 to 0.75
- top_coupling: bfloat16 [63, 6, 32, 32], replicated, as said below
- top_far: int32 [63, 6], replicated, may hold values from 0 to 31, as said below
Outputs:
- product: bfloat16 [64, 524288], P('rhs', 'leaf')
The draws below stay inside these ranges and needn't reach their ends.
Inputs may be any that keep to these rules, and one draw needn't show every extreme that they name: near_list[g, 0] is g; every entry lies within 64 leaves of g. `inner_far`: an entry for a cluster of level l names a cluster of the same level within 64 / 2^l of it. `top_far`: an entry names a cluster of the same level. `inner_coupling`: independent real entries. `top_coupling`: independent real entries.
All inputs are finite; a program needn't handle non-finite values.
Results may differ from the reference program's by a relative error of at most 0.024.
Values may be sent and summed in bfloat16 or wider, within the bound.
A program may use at most 128 MiB of HBM per device.

```python
import math
import jax
import jax.numpy as jnp
from jax import lax

LEAF = 128
RANK = 32
NEAR = 4
FAR = 6
DEPTH = 6
LD = 64
NODES_DEV = 127
NODES = 8128
NLEAF = 4096
NPTS = 524288
COLS = 64
TOPN = 63
TOPE = 62
N_LEAF = 64


def inner_heights(nodes_dev, leaves, node_total):
    within = jnp.arange(node_total, dtype=jnp.int32) % nodes_dev
    height = jnp.zeros((node_total,), jnp.int32)
    for bit_index in range(1, leaves.bit_length()):
        height = height + (within >= 2 * leaves - (2 * leaves >> bit_index)).astype(jnp.int32)
    return (within, height)


def top_heights(node_total):
    devices = node_total + 1
    within = jnp.arange(node_total, dtype=jnp.int32)
    height = jnp.ones((node_total,), jnp.int32)
    for bit_index in range(1, devices.bit_length() - 1):
        height = height + (within >= devices - (devices >> bit_index)).astype(jnp.int32)
    return height


def draw_near_list(key, part):
    key = jax.random.fold_in(key, 11)
    leaf_ids = jnp.arange(NLEAF, dtype=jnp.int32)[:, None]
    drawn = jax.random.randint(key, (NLEAF, NEAR), -LD, LD + 1)
    entry_id = jnp.arange(NEAR, dtype=jnp.int32)[None, :]
    jumps_drawn = jnp.where(entry_id == 0, 0, jnp.where(entry_id == 1, LD, jnp.where(entry_id == 2, -LD, drawn)))
    return jnp.clip(leaf_ids + jumps_drawn, 0, NLEAF - 1).astype(jnp.int32)


def draw_inner_far(key, part):
    key = jax.random.fold_in(key, 21)
    within, height = inner_heights(NODES_DEV, LD, NODES)
    device = jnp.arange(NODES, dtype=jnp.int32) // NODES_DEV
    node_count = jnp.right_shift(jnp.full((NODES,), LD, jnp.int32), height)
    local_id = within - (2 * LD - 2 * node_count)
    global_id = device * node_count + local_id
    level_total = NODES // NODES_DEV * node_count
    drawn = jax.random.randint(key, (NODES, FAR), 0, 1 << 20) % (2 * node_count[:, None] + 1) - node_count[:, None]
    entry_id = jnp.arange(FAR, dtype=jnp.int32)[None, :]
    jumps_drawn = jnp.where(entry_id == 0, node_count[:, None], jnp.where(entry_id == 1, -node_count[:, None], drawn))
    return jnp.clip(global_id[:, None] + jumps_drawn, 0, level_total[:, None] - 1).astype(jnp.int32)


def draw_top_far(key, part):
    key = jax.random.fold_in(key, 41)
    height = top_heights(TOPN)
    node_count = jnp.right_shift(jnp.full((TOPN,), TOPN + 1, jnp.int32), height)
    drawn = jax.random.randint(key, (TOPN, FAR), 0, 1 << 20) % node_count[:, None]
    return drawn.at[0, 0].set((TOPN + 1) // 2 - 1).astype(jnp.int32)


def draw_inner_coupling(key, part):
    key = jax.random.fold_in(key, 31)
    within, height = inner_heights(NODES_DEV, LD, NODES)
    scale = jnp.sqrt(2.0) ** height.astype(jnp.float32) / math.sqrt(FAR * RANK)
    values = jnp.clip(jax.random.normal(key, (NODES, FAR, RANK, RANK), jnp.float32), -6.0, 6.0)
    return (values * scale[:, None, None, None]).astype(jnp.bfloat16)


def draw_top_coupling(key, part):
    key = jax.random.fold_in(key, 51)
    height = top_heights(TOPN)
    scale = jnp.sqrt(2.0) ** (height + DEPTH).astype(jnp.float32) / math.sqrt(FAR * RANK)
    values = jnp.clip(jax.random.normal(key, (TOPN, FAR, RANK, RANK), jnp.float32), -6.0, 6.0)
    return (values * scale[:, None, None, None]).astype(jnp.bfloat16)


def levels(stream_key, extent, cuts, low, top_value):
    gain = 1.0
    for axis_at, shards_of in cuts:
        draws = jax.random.uniform(jax.random.fold_in(jax.random.fold_in(stream_key, 6), axis_at), (shards_of,), jnp.float32, low / len(cuts), top_value / len(cuts))
        gain = gain * jnp.repeat(jnp.exp(draws), extent[axis_at] // shards_of).reshape((-1,) + (1,) * (len(extent) - 1 - axis_at))
    return gain


def normal_values(key, shape, deviation, limit, cuts=(), held_as=jnp.bfloat16):
    result = deviation * jax.random.normal(key, shape, jnp.float32)
    if cuts:
        result = result * levels(key, shape, cuts, -0.22, 0.18)
    return jnp.clip(result, -limit, limit).astype(held_as)


def setup_inputs(seed: int = 0) -> dict:
    arg_keys = jax.random.split(jax.random.key(seed), 11)
    rhs_cols = normal_values(arg_keys[0], (COLS, NPTS), 1.0, 6.0, ((0, 4), (1, 64)))
    near_blocks = normal_values(arg_keys[1], (NLEAF, NEAR, LEAF, LEAF), (LEAF * NEAR) ** -0.5, 0.25, ((0, 64),))
    near_list = draw_near_list(jax.random.fold_in(arg_keys[10], 71), 0)
    leaf_basis = normal_values(arg_keys[3], (NLEAF, RANK, LEAF), LEAF ** -0.5, 0.5, ((0, 64),))
    inner_transfer = normal_values(arg_keys[4], (NODES, RANK, RANK), (2 * RANK) ** -0.5, 0.75, ((0, 64),))
    inner_coupling = draw_inner_coupling(jax.random.fold_in(arg_keys[10], 71), 0)
    inner_far = draw_inner_far(jax.random.fold_in(arg_keys[10], 71), 0)
    top_transfer = normal_values(arg_keys[7], (TOPE, RANK, RANK), (2 * RANK) ** -0.5, 0.75)
    top_coupling = draw_top_coupling(jax.random.fold_in(arg_keys[10], 71), 0)
    top_far = draw_top_far(jax.random.fold_in(arg_keys[10], 71), 0)
    return {"rhs_cols": rhs_cols, "near_blocks": near_blocks, "near_list": near_list, "leaf_basis": leaf_basis, "inner_transfer": inner_transfer, "inner_coupling": inner_coupling, "inner_far": inner_far, "top_transfer": top_transfer, "top_coupling": top_coupling, "top_far": top_far}


def unpack(array, height):
    node_count = LD >> height
    offset = 2 * LD - 2 * node_count
    shaped = array.reshape((N_LEAF, NODES_DEV) + array.shape[1:])
    return shaped[:, offset:offset + node_count].reshape((N_LEAF * node_count,) + array.shape[1:])


def lift_up(transfer_maps, coeffs):
    product = jnp.einsum("kij,kjc->kic", transfer_maps.astype(jnp.float32), coeffs.astype(jnp.float32), precision=lax.Precision.HIGHEST)
    return product.reshape((-1, 2) + product.shape[1:]).sum(axis=1).astype(jnp.bfloat16)


def couple(coupling, pulled):
    return jnp.einsum("kfij,kfjc->kic", coupling.astype(jnp.float32), pulled.astype(jnp.float32), precision=lax.Precision.HIGHEST)


def descend(transfer_maps, parent):
    return jnp.einsum("kij,kic->kjc", transfer_maps.astype(jnp.float32), parent, precision=lax.Precision.HIGHEST)


def reference(rhs_cols, near_blocks, near_list, leaf_basis, inner_transfer, inner_coupling, inner_far, top_transfer, top_coupling, top_far):
    points = rhs_cols.reshape(COLS, NLEAF, LEAF)

    def near_group(pair):
        blocks, sources = pair
        pulled = points[:, sources]
        return jnp.einsum("knpq,cknq->ckp", blocks.astype(jnp.float32), pulled.astype(jnp.float32), precision=lax.Precision.HIGHEST)

    near_term = lax.map(near_group, (near_blocks.reshape(N_LEAF, LD, NEAR, LEAF, LEAF), near_list.reshape(N_LEAF, LD, NEAR)))
    near_term = jnp.moveaxis(near_term, 0, 1).reshape(COLS, NLEAF, LEAF)

    upward = [jnp.einsum("krp,ckp->krc", leaf_basis.astype(jnp.float32), points.astype(jnp.float32), precision=lax.Precision.HIGHEST).astype(jnp.bfloat16)]
    for height in range(1, DEPTH + 1):
        upward.append(lift_up(unpack(inner_transfer, height - 1), upward[-1]))
    root_maps = unpack(inner_transfer, DEPTH)
    root_term = jnp.einsum("kij,kjc->kic", root_maps.astype(jnp.float32), upward[DEPTH].astype(jnp.float32), precision=lax.Precision.HIGHEST).astype(jnp.bfloat16)
    levels_top = N_LEAF.bit_length() - 1
    top_coeffs = [None, root_term.astype(jnp.float32).reshape(N_LEAF // 2, 2, RANK, COLS).sum(axis=1).astype(jnp.bfloat16)]
    for height in range(2, levels_top + 1):
        offset = N_LEAF - (N_LEAF >> (height - 2))
        top_coeffs.append(lift_up(top_transfer[offset:offset + (N_LEAF >> (height - 1))], top_coeffs[-1]))
    top_fields = [None]
    for height in range(1, levels_top + 1):
        offset = N_LEAF - (N_LEAF >> (height - 1))
        node_count = N_LEAF >> height
        partners = top_far[offset:offset + node_count]
        top_fields.append(couple(top_coupling[offset:offset + node_count], top_coeffs[height][partners]))
    potential = top_fields[levels_top]
    for height in range(levels_top - 1, 0, -1):
        offset = N_LEAF - (N_LEAF >> (height - 1))
        potential = top_fields[height] + descend(top_transfer[offset:offset + (N_LEAF >> height)], jnp.repeat(potential, 2, axis=0))
    fields = []
    for height in range(DEPTH + 1):
        partners = unpack(inner_far, height)
        fields.append(couple(unpack(inner_coupling, height), upward[height][partners]))
    potential = fields[DEPTH] + descend(root_maps, jnp.repeat(potential, 2, axis=0))
    for height in range(DEPTH - 1, -1, -1):
        potential = fields[height] + descend(unpack(inner_transfer, height), jnp.repeat(potential, 2, axis=0))
    leaf_field = potential.astype(jnp.bfloat16)
    far_term = jnp.einsum("krp,krc->ckp", leaf_basis.astype(jnp.float32), leaf_field.astype(jnp.float32), precision=lax.Precision.HIGHEST)
    return (near_term + far_term).astype(jnp.bfloat16).reshape(COLS, NPTS)
```

```python
import functools

import jax
import jax.numpy as jnp
from jax import lax
from jax.experimental import pallas as pl
from jax.experimental.pallas import tpu as pltpu
from jax.sharding import PartitionSpec as P

MESH = pl.DeviceIdType.MESH
F32 = jnp.float32
BF16 = jnp.bfloat16
I32 = jnp.int32
CHUNKS = 8


def nt(a, b):
    return lax.dot_general(a, b, (((1,), (1,)), ((), ())), preferred_element_type=F32)


def nn(a, b):
    return lax.dot_general(a, b, (((1,), (0,)), ((), ())), preferred_element_type=F32)


def iota(shape, dim):
    return lax.broadcasted_iota(I32, shape, dim)


def ones_where(cond):
    return jnp.where(cond, 1.0, 0.0).astype(BF16)


def diagonal(rows):
    group = iota((16, 128), 1) >> 5
    out = rows[3]
    for m in (2, 1, 0):
        out = jnp.where(group == m, rows[m], out)
    return out


def top_place(t):
    return jnp.where(
        t < 32,
        (t & 7) * 4 + (t >> 3),
        jnp.where(
            t < 48,
            32 + (t & 3) * 4 + ((t - 32) >> 2),
            jnp.where(t < 56, 48 + (t & 1) * 4 + ((t - 48) >> 1), t),
        ),
    )


def top_parent(place):
    return jnp.where(
        place < 56,
        32 + (place >> 3) * 4 + (place & 3),
        jnp.where(place < 60, 60 + ((place - 56) >> 1), 62),
    )


def kernel(
    near_list,
    inner_far,
    top_far,
    rhs,
    near,
    basis_in,
    tr_in,
    cp_in,
    ttr_in,
    tcp_in,
    out,
    rhs_v,
    near_v,
    basis,
    tr,
    cp,
    ttr,
    tcp,
    ext,
    acc,
    w32,
    w,
    wrep,
    s32,
    s,
    se32,
    rep,
    own_mask,
    top_mask,
    cfx,
    cfe,
    field,
    roots,
    topc,
    tope,
    loc,
    rhs_send,
    rhs_recv,
    cf_send,
    cf_recv,
    a_send,
    a_recv,
    b_send,
    b_recv,
):
    me = lax.axis_index("leaf")
    col = lax.axis_index("rhs")
    core = me % 2
    z = (me // 2) % 8
    y = me // 16
    slot = y * 2 + core

    def local(src, dst, k):
        copy = pltpu.make_async_copy(src, dst, loc.at[k])
        copy.start()
        return copy

    rhs_copy = local(rhs, rhs_v, 0)
    basis_copy = local(basis_in, basis, 1)
    tr_copy = local(tr_in, tr, 2)
    ttr_copy = local(ttr_in, ttr, 3)
    cp_copy = local(cp_in, cp, 4)
    tcp_copy = local(tcp_in, tcp, 5)
    per = 64 // CHUNKS
    near_copies = [
        local(near.at[pl.ds(per * k, per)], near_v.at[pl.ds(per * k, per)], 6 + k)
        for k in range(CHUNKS)
    ]

    right = (me + 1) % 64
    left = (me + 63) % 64

    def a_peer(k):
        other = (slot + k) % 8
        return ((other // 2) * 8 + z) * 2 + other % 2

    def b_peer(k):
        return (y * 8 + (z + k) % 8) * 2 + core

    barrier = pltpu.get_barrier_semaphore()
    for peer in [right, left] + [a_peer(k) for k in range(1, 8)] + [b_peer(k) for k in range(1, 8)]:
        pl.semaphore_signal(barrier, inc=1, device_id=(peer, col), device_id_type=MESH)

    rep[...] = ones_where(
        ((iota((128, 512), 0) >> 5) == (iota((128, 512), 1) >> 7))
        & ((iota((128, 512), 0) & 31) == (iota((128, 512), 1) & 31))
    )
    own_mask[...] = ones_where((iota((256, 127), 0) >> 5) == (iota((256, 127), 1) & 7))
    top_mask[...] = ones_where(
        (iota((256, 62), 0) >> 5) == (top_place(iota((256, 62), 1)) & 7)
    )

    pl.semaphore_wait(barrier, 16)

    own = (me % 4) * 64
    rhs_copy.wait()
    for k in range(64):
        ext[own + k] = rhs_v[:, 128 * k : 128 * k + 128]

    def remote(src, dst, send, recv, peer):
        return pltpu.make_async_remote_copy(
            src_ref=src,
            dst_ref=dst,
            send_sem=send,
            recv_sem=recv,
            device_id=(peer, col),
            device_id_type=MESH,
        )

    mine = ext.at[pl.ds(own, 64)]
    rhs_right = remote(mine, mine, rhs_send.at[0], rhs_recv.at[0], right)
    rhs_left = remote(mine, mine, rhs_send.at[1], rhs_recv.at[1], left)
    rhs_right.start()
    rhs_left.start()

    basis_copy.wait()

    def leaf_up(b, _):
        x = ext[pl.ds(own + 4 * b, 4)].reshape(64, 128)
        u = basis[pl.ds(4 * b, 4)].reshape(128, 128)
        r = nt(x, u)
        cfx[1, b] = diagonal([r[16 * m : 16 * m + 16] for m in range(4)]).astype(BF16)
        return 0

    lax.fori_loop(0, 16, leaf_up, 0, unroll=4)

    tr_copy.wait()
    ttr_copy.wait()
    own_parent = ones_where(iota((64, 127), 0) == (iota((64, 127), 1) >> 1))
    top_par = ones_where(iota((32, 62), 0) + 32 == top_parent(top_place(iota((32, 62), 1))))

    def transfer_rows(i, _):
        mine = jnp.concatenate([tr[i]] * 8, axis=0) * own_mask[...]
        r = nt(own_parent, mine)
        w32[0, pl.ds(i, 64, stride=32), :] = r[:, :128]
        w32[1, pl.ds(i, 64, stride=32), :] = r[:, 128:]
        upper = jnp.concatenate([ttr[i]] * 8, axis=0) * top_mask[...]
        r = nt(top_par, upper)
        w32[0, pl.ds(2048 + i, 32, stride=32), :] = r[:, :128]
        w32[1, pl.ds(2048 + i, 32, stride=32), :] = r[:, 128:]
        return 0

    lax.fori_loop(0, 32, transfer_rows, 0, unroll=2)

    def transfer_cast(b, _):
        rows = pl.ds(pl.multiple_of(128 * b, 128), 128)
        for h in range(2):
            w[rows, 128 * h : 128 * h + 128] = w32[h, rows, :].astype(BF16)
        return 0

    lax.fori_loop(0, 24, transfer_cast, 0, unroll=2)
    last = w[2016:2048, :]
    wrep[...] = jnp.concatenate([last] * 4, axis=0)

    def up(b):
        x = jnp.concatenate([cfx[1, 2 * b], cfx[1, 2 * b + 1]], axis=1)
        return nt(x, w[128 * b : 128 * b + 128, :]).astype(BF16)

    cfx[1, 31] = jnp.zeros((16, 128), BF16)
    for b in range(15):
        cfx[1, 16 + b] = up(b)
    cfx[1, 31] = up(15)
    cfx[1, 31] = up(15)
    root = nt(jnp.concatenate([cfx[1, 30], cfx[1, 31]], axis=1), wrep[...]).astype(BF16)
    roots[slot] = root

    a_copies = [
        remote(roots.at[slot], roots.at[slot], a_send.at[k], a_recv.at[slot], a_peer(k))
        for k in range(1, 8)
    ]
    for copy in a_copies:
        copy.start()
    cf_right = remote(cfx.at[1], cfx.at[0], cf_send.at[0], cf_recv.at[0], right)
    cf_left = remote(cfx.at[1], cfx.at[2], cf_send.at[1], cf_recv.at[1], left)
    cf_right.start()
    cf_left.start()

    cp_copy.wait()
    tcp_copy.wait()
    eye = ones_where(iota((128, 127), 0) == iota((128, 127), 1))
    level = iota((8, 63), 0) + 1
    t = iota((8, 63), 1)
    first = 64 - (128 >> level)
    chosen = ones_where(((first + (me >> level)) == t) & (level < 7))
    level = iota((8, 62), 0) + 1
    t = iota((8, 62), 1)
    first = 64 - (128 >> level)
    chosen_tr = ones_where(((first + (me >> level)) == t) & (level < 6))

    def coupling_rows(i, _):
        rows = jnp.concatenate([cp[f, i] for f in range(6)] + [jnp.zeros((64, 127), BF16)], axis=0)
        r = nt(eye, rows)
        s32[0, pl.ds(i, 128, stride=32), :] = r[:, :128]
        s32[1, pl.ds(i, 128, stride=32), :] = r[:, 128:]
        rows = jnp.concatenate([tcp[f, i] for f in range(6)] + [jnp.zeros((64, 63), BF16)], axis=0)
        r = nt(chosen, rows)
        s32[0, pl.ds(4096 + i, 8, stride=32), :] = r[:, :128]
        s32[1, pl.ds(4096 + i, 8, stride=32), :] = r[:, 128:]
        se32[pl.ds(i, 8, stride=32), :] = nt(chosen_tr, jnp.concatenate([ttr[i]] * 4, axis=0))
        return 0

    lax.fori_loop(0, 32, coupling_rows, 0, unroll=2)

    def coupling_cast(b, _):
        rows = pl.ds(pl.multiple_of(128 * b, 128), 128)
        for h in range(2):
            s[rows, 128 * h : 128 * h + 128] = s32[h, rows, :].astype(BF16)
        return 0

    lax.fori_loop(0, 34, coupling_cast, 0, unroll=2)

    for k in range(1, 8):
        source = (slot + 8 - k) % 8
        remote(
            roots.at[slot], roots.at[source], a_send.at[k], a_recv.at[source], a_peer(k)
        ).wait_recv()
    pair = [roots[2 * m].astype(F32) + roots[2 * m + 1].astype(F32) for m in range(4)]
    topc[z] = diagonal(pair).astype(BF16)
    b_copies = [
        remote(topc.at[z], topc.at[z], b_send.at[k], b_recv.at[z], b_peer(k)) for k in range(1, 8)
    ]
    for copy in b_copies:
        copy.start()

    rhs_right.wait_recv()
    rhs_left.wait_recv()

    def near_leaf(k, _):
        part = [ext[near_list[f, k] & 255] for f in range(4)]
        total = None
        for h in range(2):
            x = jnp.concatenate([part[2 * h], part[2 * h + 1]], axis=1)
            v = jnp.concatenate([near_v[k, 2 * h], near_v[k, 2 * h + 1]], axis=1)
            r = nt(x, v)
            total = r if total is None else total + r
        acc[k] = total
        return 0

    for k in range(CHUNKS):
        near_copies[k].wait()
        lax.fori_loop(per * k, per * k + per, near_leaf, 0, unroll=4)

    for k in range(1, 8):
        source = (z + 8 - k) % 8
        remote(
            topc.at[z], topc.at[source], b_send.at[k], b_recv.at[source], b_peer(k)
        ).wait_recv()

    def top_up(b):
        x = jnp.concatenate([topc[2 * b], topc[2 * b + 1]], axis=1)
        return nt(x, w[2048 + 128 * b : 2048 + 128 * b + 128, :]).astype(BF16)

    topc[15] = jnp.zeros((16, 128), BF16)
    for b in range(7):
        topc[8 + b] = top_up(b)
    topc[15] = top_up(7)
    topc[15] = top_up(7)
    for h in range(2):
        r = nn(topc[8 * h : 8 * h + 8].reshape(128, 128), rep[...]).astype(BF16)
        for u in range(8):
            for m in range(4):
                tope[32 * h + 4 * u + m] = r[16 * u : 16 * u + 16, 128 * m : 128 * m + 128]

    group = iota((16, 128), 1) >> 5

    def gathered(parts):
        lo = parts[3]
        for m in (2, 1, 0):
            lo = jnp.where(group == m, parts[m], lo)
        hi = jnp.where(group == 0, parts[4], parts[5])
        return jnp.concatenate([lo, hi], axis=1)

    potential = None
    for height in range(6, 0, -1):
        row = 64 - (128 >> height) + me // (1 << height)
        parts = []
        for f in range(6):
            g = top_far[f, row] & ((64 >> height) - 1)
            if height == 1:
                place = (g & 7) * 4 + (g >> 3)
            elif height == 2:
                place = 32 + (g & 3) * 4 + (g >> 2)
            elif height == 3:
                place = 48 + (g & 1) * 4 + (g >> 1)
            else:
                place = 64 - (128 >> height) + g
            parts.append(tope[place])
        at = 4096 + 32 * (height - 1)
        here = nt(gathered(parts), jnp.concatenate([s[at : at + 32, :]] * 4, axis=0))
        if potential is not None:
            at = 32 * (height - 1)
            here = here + nn(potential[:, :32].astype(BF16), se32[at : at + 32, :].astype(BF16))
        potential = here

    cf_right.wait_recv()
    cf_left.wait_recv()
    firsts = [0, 64, 96, 112, 120, 124, 126]
    for side in range(3):
        for h in range(4):
            r = nn(cfx[side, 8 * h : 8 * h + 8].reshape(128, 128), rep[...]).astype(BF16)
            for u in range(8):
                for m in range(4):
                    node = 32 * h + 4 * u + m
                    if node == 127:
                        continue
                    lev = max(k for k in range(7) if firsts[k] <= node)
                    place = 4 * firsts[lev] + (me + side + 3) % 4 * (64 >> lev) + node - firsts[lev]
                    cfe[place] = r[16 * u : 16 * u + 16, 128 * m : 128 * m + 128]

    def couple(first_group, count, nodes_of):
        def step(b, _):
            rows = []
            for u in range(8):
                node, lev = nodes_of(b, u)
                ring = (256 >> lev) - 1
                rows.append(
                    gathered(
                        [cfe[4 * firsts[lev] + (inner_far[f, node] & ring)] for f in range(6)]
                    )
                )
            x = jnp.concatenate(rows, axis=0)
            r = nt(x, s[pl.ds(pl.multiple_of(256 * b, 256), 256), :])
            field[2 * b] = diagonal([r[16 * m : 16 * m + 16, :128] for m in range(4)])
            field[2 * b + 1] = diagonal([r[64 + 16 * m : 80 + 16 * m, 128:] for m in range(4)])
            return 0

        lax.fori_loop(first_group, first_group + count, step, 0)

    def uniform(lev):
        return lambda b, u: (8 * b + u, lev)

    def mixed(b, u):
        node = min(120 + u, 126)
        return node, max(k for k in range(7) if firsts[k] <= node)

    couple(0, 8, uniform(0))
    couple(8, 4, uniform(1))
    couple(12, 2, uniform(2))
    couple(14, 1, uniform(3))
    couple(15, 1, mixed)

    base31 = jnp.where(group == 3, potential, field[31])
    here = base31
    for _ in range(2):
        here = base31 + nn(here.astype(BF16), w[1920:2048, :])[:, 128:]
    field[30] = field[30] + nn(here.astype(BF16), w[1920:2048, :])[:, :128]
    for b in range(14, -1, -1):
        r = nn(field[16 + b].astype(BF16), w[128 * b : 128 * b + 128, :])
        field[2 * b] = field[2 * b] + r[:, :128]
        field[2 * b + 1] = field[2 * b + 1] + r[:, 128:]

    def leaf_down(b, _):
        x = field[b]
        rows = [jnp.where(group == m, x, 0.0).astype(BF16) for m in range(4)]
        r = nn(jnp.concatenate(rows, axis=0), basis[pl.ds(4 * b, 4)].reshape(128, 128))
        for m in range(4):
            k = 4 * b + m
            out[:, pl.ds(pl.multiple_of(128 * k, 128), 128)] = (
                r[16 * m : 16 * m + 16] + acc[k]
            ).astype(BF16)
        return 0

    lax.fori_loop(0, 16, leaf_down, 0, unroll=4)

    rhs_right.wait_send()
    rhs_left.wait_send()
    cf_right.wait_send()
    cf_left.wait_send()
    for copy in a_copies + b_copies:
        copy.wait_send()


def body(
    rhs_cols,
    near_blocks,
    near_list,
    leaf_basis,
    inner_transfer,
    inner_coupling,
    inner_far,
    top_transfer,
    top_coupling,
    top_far,
):
    smem = pl.BlockSpec(memory_space=pltpu.SMEM)
    hbm = pl.BlockSpec(memory_space=pl.ANY)
    vmem = pltpu.VMEM
    dma = pltpu.SemaphoreType.DMA
    return pl.pallas_call(
        kernel,
        out_shape=jax.ShapeDtypeStruct((16, 8192), BF16),
        in_specs=[smem] * 3 + [hbm] * 7,
        out_specs=pl.BlockSpec(memory_space=vmem),
        scratch_shapes=[
            vmem((16, 8192), BF16),
            vmem((64, 4, 128, 128), BF16),
            vmem((64, 32, 128), BF16),
            vmem((32, 32, 127), BF16),
            vmem((6, 32, 32, 127), BF16),
            vmem((32, 32, 62), BF16),
            vmem((6, 32, 32, 63), BF16),
            vmem((256, 16, 128), BF16),
            vmem((64, 16, 128), F32),
            vmem((2, 3072, 128), F32),
            vmem((3072, 256), BF16),
            vmem((128, 256), BF16),
            vmem((2, 4352, 128), F32),
            vmem((4352, 256), BF16),
            vmem((256, 128), F32),
            vmem((128, 512), BF16),
            vmem((256, 127), BF16),
            vmem((256, 62), BF16),
            vmem((3, 32, 16, 128), BF16),
            vmem((512, 16, 128), BF16),
            vmem((32, 16, 128), F32),
            vmem((8, 16, 128), BF16),
            vmem((16, 16, 128), BF16),
            vmem((64, 16, 128), BF16),
            dma((6 + CHUNKS,)),
            dma((2,)),
            dma((2,)),
            dma((2,)),
            dma((2,)),
            dma((8,)),
            dma((8,)),
            dma((8,)),
            dma((8,)),
        ],
        compiler_params=pltpu.CompilerParams(
            collective_id=0, has_side_effects=True, vmem_limit_bytes=56 * 1024 * 1024
        ),
        name="h2_product",
    )(
        near_list.T,
        inner_far.T,
        top_far.T,
        rhs_cols,
        near_blocks,
        leaf_basis,
        inner_transfer.transpose(1, 2, 0),
        inner_coupling.transpose(1, 2, 3, 0),
        top_transfer.transpose(1, 2, 0),
        top_coupling.transpose(1, 2, 3, 0),
    )


def solution(mesh):
    return jax.shard_map(
        body,
        mesh=mesh,
        in_specs=(
            P("rhs", "leaf"),
            P("leaf", None, None, None),
            P("leaf", None),
            P("leaf", None, None),
            P("leaf", None, None),
            P("leaf", None, None, None),
            P("leaf", None),
            P(),
            P(),
            P(),
        ),
        out_specs=P("rhs", "leaf"),
        check_vma=False,
    )
```

```python
import functools

import jax
import jax.numpy as jnp
from jax import lax
from jax.experimental import pallas as pl
from jax.experimental.pallas import tpu as pltpu
from jax.sharding import PartitionSpec as P

MESH = pl.DeviceIdType.MESH
F32 = jnp.float32
BF16 = jnp.bfloat16
I32 = jnp.int32
CHUNKS = 8


def nt(a, b):
    return lax.dot_general(a, b, (((1,), (1,)), ((), ())), preferred_element_type=F32)


def nn(a, b):
    return lax.dot_general(a, b, (((1,), (0,)), ((), ())), preferred_element_type=F32)


def iota(shape, dim):
    return lax.broadcasted_iota(I32, shape, dim)


def ones_where(cond):
    return jnp.where(cond, 1.0, 0.0).astype(BF16)


def lanes_of(rows, key):
    out = rows[7]
    for m in range(7):
        out = jnp.where(key == m, rows[m], out)
    return out


def eighths(r):
    return [r[16 * m : 16 * m + 16] for m in range(8)]


def top_place(t):
    return jnp.where(
        t < 32,
        (t & 7) * 4 + (t >> 3),
        jnp.where(
            t < 48,
            32 + (t & 3) * 4 + ((t - 32) >> 2),
            jnp.where(t < 56, 48 + (t & 1) * 4 + ((t - 48) >> 1), t),
        ),
    )


def top_parent(place):
    return jnp.where(
        place < 56,
        32 + (place >> 3) * 4 + (place & 3),
        jnp.where(place < 60, 60 + ((place - 56) >> 1), 62),
    )


def kernel(
    near_list,
    inner_far,
    top_far,
    rhs,
    near,
    basis_in,
    tr_in,
    cp_in,
    ttr_in,
    tcp_in,
    out,
    rhs_v,
    near_v,
    basis,
    tr,
    cp,
    ttr,
    tcp,
    trf,
    ttrf,
    ext,
    acc,
    w,
    wtop,
    wrep,
    s,
    stop,
    etop,
    perm,
    rep,
    cfx,
    cfe,
    field,
    roots,
    topz,
    topc,
    tope,
    loc,
    rhs_send,
    rhs_recv,
    cf_send,
    cf_recv,
    a_send,
    a_recv,
    b_send,
    b_recv,
):
    me = lax.axis_index("leaf")
    col = lax.axis_index("rhs")
    core = me % 2
    z = (me // 2) % 8
    y = me // 16
    slot = y * 2 + core

    def local(src, dst, k):
        copy = pltpu.make_async_copy(src, dst, loc.at[k])
        copy.start()
        return copy

    rhs_copy = local(rhs, rhs_v, 0)
    basis_copy = local(basis_in, basis, 1)
    tr_copy = local(tr_in, tr, 2)
    ttr_copy = local(ttr_in, ttr, 3)
    cp_copy = local(cp_in, cp, 4)
    tcp_copy = local(tcp_in, tcp, 5)
    per = 64 // CHUNKS
    near_copies = [
        local(near.at[pl.ds(per * k, per)], near_v.at[pl.ds(per * k, per)], 6 + k)
        for k in range(CHUNKS)
    ]

    right = (me + 1) % 64
    left = (me + 63) % 64

    def a_peer(k):
        other = (slot + k) % 8
        return ((other // 2) * 8 + z) * 2 + other % 2

    def b_peer(k):
        return (y * 8 + (z + k) % 8) * 2 + core

    barrier = pltpu.get_barrier_semaphore()
    for peer in [right, left] + [a_peer(k) for k in range(1, 8)] + [b_peer(k) for k in range(1, 8)]:
        pl.semaphore_signal(barrier, inc=1, device_id=(peer, col), device_id_type=MESH)

    row, lane = iota((256, 256), 0), iota((256, 256), 1)
    perm[...] = ones_where(((row >> 5) == (lane & 7)) & ((row & 31) == (lane >> 3)))
    row, lane = iota((256, 1024), 0), iota((256, 1024), 1)
    rep[...] = ones_where(((row >> 3) == (lane & 31)) & ((row & 7) == (lane >> 7)))
    lane = iota((16, 256), 1)
    octet_key = lane & 7
    group_key = lane >> 5

    pl.semaphore_wait(barrier, 16)

    own = (me % 4) * 64
    rhs_copy.wait()
    for k in range(64):
        ext[own + k] = rhs_v[:, 128 * k : 128 * k + 128]

    def remote(src, dst, send, recv, peer):
        return pltpu.make_async_remote_copy(
            src_ref=src,
            dst_ref=dst,
            send_sem=send,
            recv_sem=recv,
            device_id=(peer, col),
            device_id_type=MESH,
        )

    mine = ext.at[pl.ds(own, 64)]
    rhs_right = remote(mine, mine, rhs_send.at[0], rhs_recv.at[0], right)
    rhs_left = remote(mine, mine, rhs_send.at[1], rhs_recv.at[1], left)
    rhs_right.start()
    rhs_left.start()

    basis_copy.wait()

    def leaf_up(b, _):
        x = ext[pl.ds(own + 8 * b, 8)].reshape(128, 128)
        u = basis[pl.ds(8 * b, 8)].reshape(256, 128)
        cfx[1, b] = lanes_of(eighths(nt(x, u)), group_key).astype(BF16)
        return 0

    lax.fori_loop(0, 8, leaf_up, 0, unroll=4)
    ordered = nn(cfx[1, 0:8].reshape(128, 256), perm[...]).astype(BF16)
    for b in range(8):
        cfx[1, b] = ordered[16 * b : 16 * b + 16]

    tr_copy.wait()
    ttr_copy.wait()
    own_parent = ones_where(iota((64, 127), 0) == (iota((64, 127), 1) >> 1))
    top_par = ones_where(iota((32, 62), 0) + 32 == top_parent(top_place(iota((32, 62), 1))))
    own_mask = ones_where(iota((8, 127), 0) == (iota((8, 127), 1) & 7)).astype(F32)
    top_mask = ones_where(iota((8, 62), 0) == (top_place(iota((8, 62), 1)) & 7)).astype(F32)
    level = (iota((40, 62), 0) >> 3) + 1
    chosen_tr = ones_where(
        (64 - (128 >> level) + (me >> level) == iota((40, 62), 1)) & ((iota((40, 62), 0) & 7) == 0)
    )
    trf[...] = tr[...].astype(F32)
    ttrf[...] = ttr[...].astype(F32)

    def spread(ref, i, mask, width):
        rows = []
        for j in range(32):
            x = jnp.broadcast_to(ref[i, j : j + 1, :], (8, width))
            rows.append(x if mask is None else x * mask)
        return jnp.concatenate(rows, axis=0).astype(BF16)

    def put(dst, at, pair, count):
        for g in range(count):
            both = [r[8 * g : 8 * g + 8] for r in pair]
            dst[g, at, :] = jnp.concatenate(both, axis=0).astype(BF16)

    def transfer_rows(q, _):
        at = pl.ds(pl.multiple_of(16 * q, 16), 16)
        pair = [nt(own_parent, spread(trf, 2 * q + e, own_mask, 127)) for e in range(2)]
        put(w, at, pair, 8)
        pair = [nt(top_par, spread(ttrf, 2 * q + e, top_mask, 62)) for e in range(2)]
        put(wtop, at, pair, 4)
        return 0

    lax.fori_loop(0, 16, transfer_rows, 0)
    row, lane = iota((128, 256), 0), iota((128, 256), 1)
    root_rows = ones_where((lane & 7 == 7) & ((lane >> 3) == (row & 31)))
    wrep[...] = nn(root_rows, w[7]).astype(BF16)

    low = octet_key < 4

    def up(x0, x1, mat):
        r = nt(jnp.concatenate([x0, x1], axis=0), mat)
        return jnp.where(low, r[:16], r[16:]).astype(BF16)

    for b in range(7):
        cfx[1, 8 + b] = up(cfx[1, 2 * b], cfx[1, 2 * b + 1], w[b])
    last = jnp.zeros((16, 256), BF16)
    for _ in range(3):
        last = up(cfx[1, 14], last, w[7])
    cfx[1, 15] = last
    roots[slot] = nt(last, wrep[...]).astype(BF16)

    a_copies = [
        remote(roots.at[slot], roots.at[slot], a_send.at[k], a_recv.at[slot], a_peer(k))
        for k in range(1, 8)
    ]
    for copy in a_copies:
        copy.start()
    cf_right = remote(cfx.at[1], cfx.at[0], cf_send.at[0], cf_recv.at[0], right)
    cf_left = remote(cfx.at[1], cfx.at[2], cf_send.at[1], cf_recv.at[1], left)
    cf_right.start()
    cf_left.start()

    cp_copy.wait()
    tcp_copy.wait()
    eye = ones_where(iota((128, 127), 0) == iota((128, 127), 1))
    level = (iota((48, 63), 0) >> 3) + 1
    chosen = ones_where(64 - (128 >> level) + (me >> level) == iota((48, 63), 1))

    def slab(ref, i, width):
        return jnp.concatenate(
            [ref[f, i] for f in range(6)] + [jnp.zeros((64, width), BF16)], axis=0
        )

    def coupling_rows(q, _):
        at = pl.ds(pl.multiple_of(16 * q, 16), 16)
        put(s, at, [nt(eye, slab(cp, 2 * q + e, 127)) for e in range(2)], 16)
        put(stop, at, [nt(chosen, slab(tcp, 2 * q + e, 63)) for e in range(2)], 6)
        pair = [nt(chosen_tr, spread(ttrf, 2 * q + e, None, 62)) for e in range(2)]
        put(etop, at, pair, 5)
        return 0

    lax.fori_loop(0, 16, coupling_rows, 0)

    for k in range(1, 8):
        source = (slot + 8 - k) % 8
        remote(
            roots.at[slot], roots.at[source], a_send.at[k], a_recv.at[source], a_peer(k)
        ).wait_recv()
    packed = None
    for m in (3, 2, 1, 0):
        pair = roots[2 * m].astype(F32) + roots[2 * m + 1].astype(F32)
        packed = pair if packed is None else jnp.where(group_key[:, :128] == m, pair, packed)
    topz[z] = packed.astype(BF16)
    b_copies = [
        remote(topz.at[z], topz.at[z], b_send.at[k], b_recv.at[z], b_peer(k)) for k in range(1, 8)
    ]
    for copy in b_copies:
        copy.start()

    rhs_right.wait_recv()
    rhs_left.wait_recv()

    def near_leaf(k, _):
        part = [ext[near_list[f, k] & 255] for f in range(4)]
        total = None
        for h in range(2):
            x = jnp.concatenate([part[2 * h], part[2 * h + 1]], axis=1)
            v = jnp.concatenate([near_v[k, 2 * h], near_v[k, 2 * h + 1]], axis=1)
            r = nt(x, v)
            total = r if total is None else total + r
        acc[k] = total
        return 0

    for k in range(CHUNKS):
        near_copies[k].wait()
        lax.fori_loop(per * k, per * k + per, near_leaf, 0, unroll=4)

    for k in range(1, 8):
        source = (z + 8 - k) % 8
        remote(
            topz.at[z], topz.at[source], b_send.at[k], b_recv.at[source], b_peer(k)
        ).wait_recv()
    pairs = [jnp.concatenate([topz[2 * h], topz[2 * h + 1]], axis=1) for h in range(4)]
    ordered = nn(jnp.concatenate(pairs, axis=0), perm[...]).astype(BF16)
    for b in range(4):
        topc[b] = ordered[16 * b : 16 * b + 16]
    for b in range(3):
        topc[4 + b] = up(topc[2 * b], topc[2 * b + 1], wtop[b])
    last = jnp.zeros((16, 256), BF16)
    for _ in range(3):
        last = up(topc[6], last, wtop[3])
    topc[7] = last
    r = nn(topc[...].reshape(128, 256), rep[...]).astype(BF16)
    for b in range(8):
        for m in range(8):
            tope[8 * b + m] = r[16 * b : 16 * b + 16, 128 * m : 128 * m + 128]

    group = group_key[:, :128]

    def gathered(parts):
        lo = parts[3]
        for m in (2, 1, 0):
            lo = jnp.where(group == m, parts[m], lo)
        hi = jnp.where(group == 0, parts[4], parts[5])
        return jnp.concatenate([lo, hi], axis=1)

    potential = None
    for height in range(6, 0, -1):
        node = 64 - (128 >> height) + me // (1 << height)
        parts = []
        for f in range(6):
            g = top_far[f, node] & ((64 >> height) - 1)
            if height == 1:
                place = (g & 7) * 4 + (g >> 3)
            elif height == 2:
                place = 32 + (g & 3) * 4 + (g >> 2)
            elif height == 3:
                place = 48 + (g & 1) * 4 + (g >> 1)
            else:
                place = 64 - (128 >> height) + g
            parts.append(tope[place])
        here = nt(gathered(parts), stop[height - 1])
        if potential is not None:
            here = here + nn(potential.astype(BF16), etop[height - 1])
        potential = here

    cf_right.wait_recv()
    cf_left.wait_recv()
    firsts = [0, 64, 96, 112, 120, 124, 126]
    for side in range(3):
        for h in range(2):
            r = nn(cfx[side, 8 * h : 8 * h + 8].reshape(128, 256), rep[...]).astype(BF16)
            for u in range(8):
                for m in range(8):
                    node = 64 * h + 8 * u + m
                    if node == 127:
                        continue
                    lev = max(k for k in range(7) if firsts[k] <= node)
                    place = 4 * firsts[lev] + (me + side + 3) % 4 * (64 >> lev) + node - firsts[lev]
                    cfe[place] = r[16 * u : 16 * u + 16, 128 * m : 128 * m + 128]

    def couple(first_group, count, nodes_of):
        def step(b, _):
            rows = []
            for u in range(8):
                node, lev = nodes_of(b, u)
                ring = (256 >> lev) - 1
                rows.append(
                    gathered(
                        [cfe[4 * firsts[lev] + (inner_far[f, node] & ring)] for f in range(6)]
                    )
                )
            r = nt(jnp.concatenate(rows, axis=0), s[b])
            field[b] = lanes_of(eighths(r), octet_key)
            return 0

        lax.fori_loop(first_group, first_group + count, step, 0)

    def uniform(lev):
        return lambda b, u: (8 * b + u, lev)

    def mixed(b, u):
        node = min(120 + u, 126)
        return node, max(k for k in range(7) if firsts[k] <= node)

    couple(0, 8, uniform(0))
    couple(8, 4, uniform(1))
    couple(12, 2, uniform(2))
    couple(14, 1, uniform(3))
    couple(15, 1, mixed)

    def down(x, mat):
        lower = jnp.where(low, x, 0.0).astype(BF16)
        upper = jnp.where(low, 0.0, x).astype(BF16)
        r = nn(jnp.concatenate([lower, upper], axis=0), mat)
        return r[:16], r[16:]

    base = jnp.where(octet_key == 7, potential, field[15])
    here = base
    for _ in range(3):
        here = base + down(here, w[7])[1]
    field[14] = field[14] + down(here, w[7])[0]
    for b in range(6, -1, -1):
        r0, r1 = down(field[8 + b], w[b])
        field[2 * b] = field[2 * b] + r0
        field[2 * b + 1] = field[2 * b + 1] + r1
    ordered = nt(field[0:8].reshape(128, 256).astype(BF16), perm[...])

    for b in range(8):
        x = ordered[16 * b : 16 * b + 16]
        rows = [jnp.where(group_key == m, x, 0.0).astype(BF16) for m in range(8)]
        r = nn(jnp.concatenate(rows, axis=0), basis[8 * b : 8 * b + 8].reshape(256, 128))
        for m in range(8):
            k = 8 * b + m
            out[:, 128 * k : 128 * k + 128] = (r[16 * m : 16 * m + 16] + acc[k]).astype(BF16)

    rhs_right.wait_send()
    rhs_left.wait_send()
    cf_right.wait_send()
    cf_left.wait_send()
    for copy in a_copies + b_copies:
        copy.wait_send()


def body(
    rhs_cols,
    near_blocks,
    near_list,
    leaf_basis,
    inner_transfer,
    inner_coupling,
    inner_far,
    top_transfer,
    top_coupling,
    top_far,
):
    smem = pl.BlockSpec(memory_space=pltpu.SMEM)
    hbm = pl.BlockSpec(memory_space=pl.ANY)
    vmem = pltpu.VMEM
    dma = pltpu.SemaphoreType.DMA
    return pl.pallas_call(
        kernel,
        out_shape=jax.ShapeDtypeStruct((16, 8192), BF16),
        in_specs=[smem] * 3 + [hbm] * 7,
        out_specs=pl.BlockSpec(memory_space=vmem),
        scratch_shapes=[
            vmem((16, 8192), BF16),
            vmem((64, 4, 128, 128), BF16),
            vmem((64, 32, 128), BF16),
            vmem((32, 32, 127), BF16),
            vmem((6, 32, 32, 127), BF16),
            vmem((32, 32, 62), BF16),
            vmem((6, 32, 32, 63), BF16),
            vmem((32, 32, 127), F32),
            vmem((32, 32, 62), F32),
            vmem((256, 16, 128), BF16),
            vmem((64, 16, 128), F32),
            vmem((8, 256, 256), BF16),
            vmem((4, 256, 256), BF16),
            vmem((128, 256), BF16),
            vmem((16, 256, 256), BF16),
            vmem((6, 256, 256), BF16),
            vmem((5, 256, 256), BF16),
            vmem((256, 256), BF16),
            vmem((256, 1024), BF16),
            vmem((3, 16, 16, 256), BF16),
            vmem((512, 16, 128), BF16),
            vmem((16, 16, 256), F32),
            vmem((8, 16, 128), BF16),
            vmem((8, 16, 128), BF16),
            vmem((8, 16, 256), BF16),
            vmem((64, 16, 128), BF16),
            dma((6 + CHUNKS,)),
            dma((2,)),
            dma((2,)),
            dma((2,)),
            dma((2,)),
            dma((8,)),
            dma((8,)),
            dma((8,)),
            dma((8,)),
        ],
        compiler_params=pltpu.CompilerParams(
            collective_id=0, has_side_effects=True, vmem_limit_bytes=56 * 1024 * 1024
        ),
        name="h2_product",
    )(
        near_list.T,
        inner_far.T,
        top_far.T,
        rhs_cols,
        near_blocks,
        leaf_basis,
        inner_transfer.transpose(1, 2, 0),
        inner_coupling.transpose(1, 2, 3, 0),
        top_transfer.transpose(1, 2, 0),
        top_coupling.transpose(1, 2, 3, 0),
    )


def solution(mesh):
    return jax.shard_map(
        body,
        mesh=mesh,
        in_specs=(
            P("rhs", "leaf"),
            P("leaf", None, None, None),
            P("leaf", None),
            P("leaf", None, None),
            P("leaf", None, None),
            P("leaf", None, None, None),
            P("leaf", None),
            P(),
            P(),
            P(),
        ),
        out_specs=P("rhs", "leaf"),
        check_vma=False,
    )
```

```python
import functools

import jax
import jax.numpy as jnp
from jax import lax
from jax.experimental import pallas as pl
from jax.experimental.pallas import tpu as pltpu
from jax.sharding import PartitionSpec as P

MESH = pl.DeviceIdType.MESH
F32 = jnp.float32
BF16 = jnp.bfloat16
I32 = jnp.int32
CHUNKS = 4


def nt(a, b):
    return lax.dot_general(a, b, (((1,), (1,)), ((), ())), preferred_element_type=F32)


def nn(a, b):
    return lax.dot_general(a, b, (((1,), (0,)), ((), ())), preferred_element_type=F32)


def iota(shape, dim):
    return lax.broadcasted_iota(I32, shape, dim)


def ones_where(cond):
    return jnp.where(cond, 1.0, 0.0).astype(BF16)


def lanes_of(rows, key):
    out = rows[7]
    for m in range(7):
        out = jnp.where(key == m, rows[m], out)
    return out


def eighths(r):
    return [r[16 * m : 16 * m + 16] for m in range(8)]


def top_place(t):
    return jnp.where(
        t < 32,
        (t & 7) * 4 + (t >> 3),
        jnp.where(
            t < 48,
            32 + (t & 3) * 4 + ((t - 32) >> 2),
            jnp.where(t < 56, 48 + (t & 1) * 4 + ((t - 48) >> 1), t),
        ),
    )


def top_parent(place):
    return jnp.where(
        place < 56,
        32 + (place >> 3) * 4 + (place & 3),
        jnp.where(place < 60, 60 + ((place - 56) >> 1), 62),
    )


def kernel(
    near_list,
    inner_far,
    top_far,
    rhs,
    near,
    basis_in,
    tr_in,
    cp_in,
    ttr_in,
    tcp_in,
    out,
    rhs_v,
    near_v,
    basis,
    tr,
    cp,
    ttr,
    tcp,
    trf,
    ttrf,
    ext,
    acc,
    w,
    wtop,
    wrep,
    s,
    stop,
    etop,
    perm,
    rep,
    cfx,
    cfe,
    field,
    roots,
    topz,
    topc,
    tope,
    loc,
    rhs_send,
    rhs_recv,
    cf_send,
    cf_recv,
    a_send,
    a_recv,
    b_send,
    b_recv,
):
    me = lax.axis_index("leaf")
    col = lax.axis_index("rhs")
    core = me % 2
    z = (me // 2) % 8
    y = me // 16
    slot = y * 2 + core

    def local(src, dst, k):
        copy = pltpu.make_async_copy(src, dst, loc.at[k])
        copy.start()
        return copy

    rhs_copy = local(rhs, rhs_v, 0)
    basis_copy = local(basis_in, basis, 1)
    tr_copy = local(tr_in, tr, 2)
    ttr_copy = local(ttr_in, ttr, 3)
    cp_copy = local(cp_in, cp, 4)
    tcp_copy = local(tcp_in, tcp, 5)
    per = 64 // CHUNKS
    near_copies = [
        local(near.at[pl.ds(per * k, per)], near_v.at[pl.ds(per * k, per)], 6 + k)
        for k in range(CHUNKS)
    ]

    right = (me + 1) % 64
    left = (me + 63) % 64

    def a_peer(k):
        other = (slot + k) % 8
        return ((other // 2) * 8 + z) * 2 + other % 2

    def b_peer(k):
        return (y * 8 + (z + k) % 8) * 2 + core

    barrier = pltpu.get_barrier_semaphore()
    for peer in [right, left] + [a_peer(k) for k in range(1, 8)] + [b_peer(k) for k in range(1, 8)]:
        pl.semaphore_signal(barrier, inc=1, device_id=(peer, col), device_id_type=MESH)

    row, lane = iota((256, 256), 0), iota((256, 256), 1)
    perm[...] = ones_where(((row >> 5) == (lane & 7)) & ((row & 31) == (lane >> 3)))
    row, lane = iota((256, 1024), 0), iota((256, 1024), 1)
    rep[...] = ones_where(((row >> 3) == (lane & 31)) & ((row & 7) == (lane >> 7)))
    lane = iota((16, 256), 1)
    octet_key = lane & 7
    group_key = lane >> 5

    pl.semaphore_wait(barrier, 16)

    own = (me % 4) * 64
    rhs_copy.wait()
    for k in range(64):
        ext[own + k] = rhs_v[:, 128 * k : 128 * k + 128]

    def remote(src, dst, send, recv, peer):
        return pltpu.make_async_remote_copy(
            src_ref=src,
            dst_ref=dst,
            send_sem=send,
            recv_sem=recv,
            device_id=(peer, col),
            device_id_type=MESH,
        )

    mine = ext.at[pl.ds(own, 64)]
    rhs_right = remote(mine, mine, rhs_send.at[0], rhs_recv.at[0], right)
    rhs_left = remote(mine, mine, rhs_send.at[1], rhs_recv.at[1], left)
    rhs_right.start()
    rhs_left.start()

    basis_copy.wait()

    def leaf_up(b, _):
        x = ext[pl.ds(own + 8 * b, 8)].reshape(128, 128)
        u = basis[pl.ds(8 * b, 8)].reshape(256, 128)
        cfx[1, b] = lanes_of(eighths(nt(x, u)), group_key).astype(BF16)
        return 0

    lax.fori_loop(0, 8, leaf_up, 0, unroll=8)
    ordered = nn(cfx[1, 0:8].reshape(128, 256), perm[...]).astype(BF16)
    for b in range(8):
        cfx[1, b] = ordered[16 * b : 16 * b + 16]

    tr_copy.wait()
    ttr_copy.wait()
    own_parent = ones_where(iota((64, 127), 0) == (iota((64, 127), 1) >> 1))
    top_par = ones_where(iota((32, 62), 0) + 32 == top_parent(top_place(iota((32, 62), 1))))
    own_mask = ones_where(iota((8, 127), 0) == (iota((8, 127), 1) & 7)).astype(F32)
    top_mask = ones_where(iota((8, 62), 0) == (top_place(iota((8, 62), 1)) & 7)).astype(F32)
    level = (iota((40, 62), 0) >> 3) + 1
    chosen_tr = ones_where(
        (64 - (128 >> level) + (me >> level) == iota((40, 62), 1)) & ((iota((40, 62), 0) & 7) == 0)
    )
    trf[...] = tr[...].astype(F32)
    ttrf[...] = ttr[...].astype(F32)

    def spread(ref, i, mask, width):
        rows = []
        for j in range(32):
            x = jnp.broadcast_to(ref[i, j : j + 1, :], (8, width))
            rows.append(x if mask is None else x * mask)
        return jnp.concatenate(rows, axis=0).astype(BF16)

    def put(dst, at, pair, count):
        for g in range(count):
            both = [r[8 * g : 8 * g + 8] for r in pair]
            dst[g, at, :] = jnp.concatenate(both, axis=0).astype(BF16)

    def transfer_rows(q, _):
        at = pl.ds(pl.multiple_of(16 * q, 16), 16)
        pair = [nt(own_parent, spread(trf, 2 * q + e, own_mask, 127)) for e in range(2)]
        put(w, at, pair, 8)
        pair = [nt(top_par, spread(ttrf, 2 * q + e, top_mask, 62)) for e in range(2)]
        put(wtop, at, pair, 4)
        return 0

    lax.fori_loop(0, 16, transfer_rows, 0, unroll=8)
    row, lane = iota((128, 256), 0), iota((128, 256), 1)
    root_rows = ones_where((lane & 7 == 7) & ((lane >> 3) == (row & 31)))
    wrep[...] = nn(root_rows, w[7]).astype(BF16)

    low = octet_key < 4

    def up(x0, x1, mat):
        r = nt(jnp.concatenate([x0, x1], axis=0), mat)
        return jnp.where(low, r[:16], r[16:]).astype(BF16)

    for b in range(7):
        cfx[1, 8 + b] = up(cfx[1, 2 * b], cfx[1, 2 * b + 1], w[b])
    last = jnp.zeros((16, 256), BF16)
    for _ in range(3):
        last = up(cfx[1, 14], last, w[7])
    cfx[1, 15] = last
    roots[slot] = nt(last, wrep[...]).astype(BF16)

    a_copies = [
        remote(roots.at[slot], roots.at[slot], a_send.at[k], a_recv.at[slot], a_peer(k))
        for k in range(1, 8)
    ]
    for copy in a_copies:
        copy.start()
    cf_right = remote(cfx.at[1], cfx.at[0], cf_send.at[0], cf_recv.at[0], right)
    cf_left = remote(cfx.at[1], cfx.at[2], cf_send.at[1], cf_recv.at[1], left)
    cf_right.start()
    cf_left.start()

    cp_copy.wait()
    tcp_copy.wait()
    eye = ones_where(iota((128, 127), 0) == iota((128, 127), 1))
    level = (iota((48, 63), 0) >> 3) + 1
    chosen = ones_where(64 - (128 >> level) + (me >> level) == iota((48, 63), 1))

    def slab(ref, i, width):
        return jnp.concatenate(
            [ref[f, i] for f in range(6)] + [jnp.zeros((64, width), BF16)], axis=0
        )

    def coupling_rows(q, _):
        at = pl.ds(pl.multiple_of(16 * q, 16), 16)
        put(s, at, [nt(eye, slab(cp, 2 * q + e, 127)) for e in range(2)], 16)
        put(stop, at, [nt(chosen, slab(tcp, 2 * q + e, 63)) for e in range(2)], 6)
        pair = [nt(chosen_tr, spread(ttrf, 2 * q + e, None, 62)) for e in range(2)]
        put(etop, at, pair, 5)
        return 0

    lax.fori_loop(0, 16, coupling_rows, 0, unroll=8)

    for k in range(1, 8):
        source = (slot + 8 - k) % 8
        remote(
            roots.at[slot], roots.at[source], a_send.at[k], a_recv.at[source], a_peer(k)
        ).wait_recv()
    packed = None
    for m in (3, 2, 1, 0):
        pair = roots[2 * m].astype(F32) + roots[2 * m + 1].astype(F32)
        packed = pair if packed is None else jnp.where(group_key[:, :128] == m, pair, packed)
    topz[z] = packed.astype(BF16)
    b_copies = [
        remote(topz.at[z], topz.at[z], b_send.at[k], b_recv.at[z], b_peer(k)) for k in range(1, 8)
    ]
    for copy in b_copies:
        copy.start()

    rhs_right.wait_recv()
    rhs_left.wait_recv()

    def near_leaf(k, _):
        part = [ext[near_list[f, k] & 255] for f in range(4)]
        total = None
        for h in range(2):
            x = jnp.concatenate([part[2 * h], part[2 * h + 1]], axis=1)
            v = jnp.concatenate([near_v[k, 2 * h], near_v[k, 2 * h + 1]], axis=1)
            r = nt(x, v)
            total = r if total is None else total + r
        acc[k] = total
        return 0

    for k in range(CHUNKS):
        near_copies[k].wait()
        lax.fori_loop(per * k, per * k + per, near_leaf, 0, unroll=16)

    for k in range(1, 8):
        source = (z + 8 - k) % 8
        remote(
            topz.at[z], topz.at[source], b_send.at[k], b_recv.at[source], b_peer(k)
        ).wait_recv()
    pairs = [jnp.concatenate([topz[2 * h], topz[2 * h + 1]], axis=1) for h in range(4)]
    ordered = nn(jnp.concatenate(pairs, axis=0), perm[...]).astype(BF16)
    for b in range(4):
        topc[b] = ordered[16 * b : 16 * b + 16]
    for b in range(3):
        topc[4 + b] = up(topc[2 * b], topc[2 * b + 1], wtop[b])
    last = jnp.zeros((16, 256), BF16)
    for _ in range(3):
        last = up(topc[6], last, wtop[3])
    topc[7] = last
    r = nn(topc[...].reshape(128, 256), rep[...]).astype(BF16)
    for b in range(8):
        for m in range(8):
            tope[8 * b + m] = r[16 * b : 16 * b + 16, 128 * m : 128 * m + 128]

    group = group_key[:, :128]

    def gathered(parts):
        lo = parts[3]
        for m in (2, 1, 0):
            lo = jnp.where(group == m, parts[m], lo)
        hi = jnp.where(group == 0, parts[4], parts[5])
        return jnp.concatenate([lo, hi], axis=1)

    potential = None
    for height in range(6, 0, -1):
        node = 64 - (128 >> height) + me // (1 << height)
        parts = []
        for f in range(6):
            g = top_far[f, node] & ((64 >> height) - 1)
            if height == 1:
                place = (g & 7) * 4 + (g >> 3)
            elif height == 2:
                place = 32 + (g & 3) * 4 + (g >> 2)
            elif height == 3:
                place = 48 + (g & 1) * 4 + (g >> 1)
            else:
                place = 64 - (128 >> height) + g
            parts.append(tope[place])
        here = nt(gathered(parts), stop[height - 1])
        if potential is not None:
            here = here + nn(potential.astype(BF16), etop[height - 1])
        potential = here

    cf_right.wait_recv()
    cf_left.wait_recv()
    firsts = [0, 64, 96, 112, 120, 124, 126]
    for side in range(3):
        for h in range(2):
            r = nn(cfx[side, 8 * h : 8 * h + 8].reshape(128, 256), rep[...]).astype(BF16)
            for u in range(8):
                for m in range(8):
                    node = 64 * h + 8 * u + m
                    if node == 127:
                        continue
                    lev = max(k for k in range(7) if firsts[k] <= node)
                    place = 4 * firsts[lev] + (me + side + 3) % 4 * (64 >> lev) + node - firsts[lev]
                    cfe[place] = r[16 * u : 16 * u + 16, 128 * m : 128 * m + 128]

    def couple(first_group, count, nodes_of):
        def step(b, _):
            rows = []
            for u in range(8):
                node, lev = nodes_of(b, u)
                ring = (256 >> lev) - 1
                rows.append(
                    gathered(
                        [cfe[4 * firsts[lev] + (inner_far[f, node] & ring)] for f in range(6)]
                    )
                )
            r = nt(jnp.concatenate(rows, axis=0), s[b])
            field[b] = lanes_of(eighths(r), octet_key)
            return 0

        lax.fori_loop(first_group, first_group + count, step, 0, unroll=count)

    def uniform(lev):
        return lambda b, u: (8 * b + u, lev)

    def mixed(b, u):
        node = min(120 + u, 126)
        return node, max(k for k in range(7) if firsts[k] <= node)

    couple(0, 8, uniform(0))
    couple(8, 4, uniform(1))
    couple(12, 2, uniform(2))
    couple(14, 1, uniform(3))
    couple(15, 1, mixed)

    def down(x, mat):
        lower = jnp.where(low, x, 0.0).astype(BF16)
        upper = jnp.where(low, 0.0, x).astype(BF16)
        r = nn(jnp.concatenate([lower, upper], axis=0), mat)
        return r[:16], r[16:]

    base = jnp.where(octet_key == 7, potential, field[15])
    here = base
    for _ in range(3):
        here = base + down(here, w[7])[1]
    field[14] = field[14] + down(here, w[7])[0]
    for b in range(6, -1, -1):
        r0, r1 = down(field[8 + b], w[b])
        field[2 * b] = field[2 * b] + r0
        field[2 * b + 1] = field[2 * b + 1] + r1
    ordered = nt(field[0:8].reshape(128, 256).astype(BF16), perm[...])

    for b in range(8):
        x = ordered[16 * b : 16 * b + 16]
        rows = [jnp.where(group_key == m, x, 0.0).astype(BF16) for m in range(8)]
        r = nn(jnp.concatenate(rows, axis=0), basis[8 * b : 8 * b + 8].reshape(256, 128))
        for m in range(8):
            k = 8 * b + m
            out[:, 128 * k : 128 * k + 128] = (r[16 * m : 16 * m + 16] + acc[k]).astype(BF16)

    rhs_right.wait_send()
    rhs_left.wait_send()
    cf_right.wait_send()
    cf_left.wait_send()
    for copy in a_copies + b_copies:
        copy.wait_send()


def body(
    rhs_cols,
    near_blocks,
    near_list,
    leaf_basis,
    inner_transfer,
    inner_coupling,
    inner_far,
    top_transfer,
    top_coupling,
    top_far,
):
    smem = pl.BlockSpec(memory_space=pltpu.SMEM)
    hbm = pl.BlockSpec(memory_space=pl.ANY)
    vmem = pltpu.VMEM
    dma = pltpu.SemaphoreType.DMA
    return pl.pallas_call(
        kernel,
        out_shape=jax.ShapeDtypeStruct((16, 8192), BF16),
        in_specs=[smem] * 3 + [hbm] * 7,
        out_specs=pl.BlockSpec(memory_space=vmem),
        scratch_shapes=[
            vmem((16, 8192), BF16),
            vmem((64, 4, 128, 128), BF16),
            vmem((64, 32, 128), BF16),
            vmem((32, 32, 127), BF16),
            vmem((6, 32, 32, 127), BF16),
            vmem((32, 32, 62), BF16),
            vmem((6, 32, 32, 63), BF16),
            vmem((32, 32, 127), F32),
            vmem((32, 32, 62), F32),
            vmem((256, 16, 128), BF16),
            vmem((64, 16, 128), F32),
            vmem((8, 256, 256), BF16),
            vmem((4, 256, 256), BF16),
            vmem((128, 256), BF16),
            vmem((16, 256, 256), BF16),
            vmem((6, 256, 256), BF16),
            vmem((5, 256, 256), BF16),
            vmem((256, 256), BF16),
            vmem((256, 1024), BF16),
            vmem((3, 16, 16, 256), BF16),
            vmem((512, 16, 128), BF16),
            vmem((16, 16, 256), F32),
            vmem((8, 16, 128), BF16),
            vmem((8, 16, 128), BF16),
            vmem((8, 16, 256), BF16),
            vmem((64, 16, 128), BF16),
            dma((6 + CHUNKS,)),
            dma((2,)),
            dma((2,)),
            dma((2,)),
            dma((2,)),
            dma((8,)),
            dma((8,)),
            dma((8,)),
            dma((8,)),
        ],
        compiler_params=pltpu.CompilerParams(
            collective_id=0, has_side_effects=True, vmem_limit_bytes=56 * 1024 * 1024
        ),
        name="h2_product",
    )(
        near_list.T,
        inner_far.T,
        top_far.T,
        rhs_cols,
        near_blocks,
        leaf_basis,
        inner_transfer.transpose(1, 2, 0),
        inner_coupling.transpose(1, 2, 3, 0),
        top_transfer.transpose(1, 2, 0),
        top_coupling.transpose(1, 2, 3, 0),
    )


def solution(mesh):
    return jax.shard_map(
        body,
        mesh=mesh,
        in_specs=(
            P("rhs", "leaf"),
            P("leaf", None, None, None),
            P("leaf", None),
            P("leaf", None, None),
            P("leaf", None, None),
            P("leaf", None, None, None),
            P("leaf", None),
            P(),
            P(),
            P(),
        ),
        out_specs=P("rhs", "leaf"),
        check_vma=False,
    )
```

```python
import functools

import jax
import jax.numpy as jnp
from jax import lax
from jax.experimental import pallas as pl
from jax.experimental.pallas import tpu as pltpu
from jax.sharding import PartitionSpec as P

MESH = pl.DeviceIdType.MESH
F32 = jnp.float32
BF16 = jnp.bfloat16
I32 = jnp.int32
CHUNKS = 4


def nt(a, b):
    return lax.dot_general(a, b, (((1,), (1,)), ((), ())), preferred_element_type=F32)


def nn(a, b):
    return lax.dot_general(a, b, (((1,), (0,)), ((), ())), preferred_element_type=F32)


def iota(shape, dim):
    return lax.broadcasted_iota(I32, shape, dim)


def ones_where(cond):
    return jnp.where(cond, 1.0, 0.0).astype(BF16)


def lanes_of(rows, key):
    out = rows[7]
    for m in range(7):
        out = jnp.where(key == m, rows[m], out)
    return out


def eighths(r):
    return [r[16 * m : 16 * m + 16] for m in range(8)]


def top_place(t):
    return jnp.where(
        t < 32,
        (t & 7) * 4 + (t >> 3),
        jnp.where(
            t < 48,
            32 + (t & 3) * 4 + ((t - 32) >> 2),
            jnp.where(t < 56, 48 + (t & 1) * 4 + ((t - 48) >> 1), t),
        ),
    )


def top_parent(place):
    return jnp.where(
        place < 56,
        32 + (place >> 3) * 4 + (place & 3),
        jnp.where(place < 60, 60 + ((place - 56) >> 1), 62),
    )


def kernel(
    near_list_in,
    inner_far_in,
    top_far_in,
    rhs,
    near,
    basis_in,
    tr_in,
    cp_in,
    ttr_in,
    tcp_in,
    out,
    rhs_v,
    near_list,
    inner_far,
    top_far,
    near_v,
    basis,
    tr,
    cp,
    ttr,
    tcp,
    trf,
    ttrf,
    ext,
    acc,
    w,
    wtop,
    wrep,
    s,
    stop,
    above_path,
    perm,
    rep,
    cfx,
    cfe,
    field,
    roots,
    topz,
    topc,
    tope,
    loc,
    rhs_send,
    rhs_recv,
    cf_send,
    cf_recv,
    a_send,
    a_recv,
    b_send,
    b_recv,
):
    me = lax.axis_index("leaf")
    col = lax.axis_index("rhs")
    core = me % 2
    z = (me // 2) % 8
    y = me // 16
    slot = y * 2 + core

    def local(src, dst, k):
        copy = pltpu.make_async_copy(src, dst, loc.at[k])
        copy.start()
        return copy

    rhs_copy = local(rhs, rhs_v, 0)
    basis_copy = local(basis_in, basis, 1)
    tr_copy = local(tr_in, tr, 2)
    ttr_copy = local(ttr_in, ttr, 3)
    cp_copy = local(cp_in, cp, 4)
    tcp_copy = local(tcp_in, tcp, 5)
    list_copies = [
        local(near_list_in, near_list, 6 + CHUNKS),
        local(inner_far_in, inner_far, 7 + CHUNKS),
        local(top_far_in, top_far, 8 + CHUNKS),
    ]
    per = 64 // CHUNKS
    near_copies = [
        local(near.at[pl.ds(per * k, per)], near_v.at[pl.ds(per * k, per)], 6 + k)
        for k in range(CHUNKS)
    ]

    right = (me + 1) % 64
    left = (me + 63) % 64

    def a_peer(k):
        other = (slot + k) % 8
        return ((other // 2) * 8 + z) * 2 + other % 2

    def b_peer(k):
        return (y * 8 + (z + k) % 8) * 2 + core

    barrier = pltpu.get_barrier_semaphore()
    for peer in [right, left] + [a_peer(k) for k in range(1, 8)] + [b_peer(k) for k in range(1, 8)]:
        pl.semaphore_signal(barrier, inc=1, device_id=(peer, col), device_id_type=MESH)

    row, lane = iota((256, 256), 0), iota((256, 256), 1)
    perm[...] = ones_where(((row >> 5) == (lane & 7)) & ((row & 31) == (lane >> 3)))
    row, lane = iota((256, 1024), 0), iota((256, 1024), 1)
    rep[...] = ones_where(((row >> 3) == (lane & 31)) & ((row & 7) == (lane >> 7)))
    lane = iota((16, 256), 1)
    octet_key = lane & 7
    group_key = lane >> 5

    pl.semaphore_wait(barrier, 16)

    own = (me % 4) * 64
    rhs_copy.wait()
    for k in range(64):
        ext[own + k] = rhs_v[:, 128 * k : 128 * k + 128]

    def remote(src, dst, send, recv, peer):
        return pltpu.make_async_remote_copy(
            src_ref=src,
            dst_ref=dst,
            send_sem=send,
            recv_sem=recv,
            device_id=(peer, col),
            device_id_type=MESH,
        )

    mine = ext.at[pl.ds(own, 64)]
    rhs_right = remote(mine, mine, rhs_send.at[0], rhs_recv.at[0], right)
    rhs_left = remote(mine, mine, rhs_send.at[1], rhs_recv.at[1], left)
    rhs_right.start()
    rhs_left.start()

    basis_copy.wait()

    def leaf_up(b, _):
        x = ext[pl.ds(own + 8 * b, 8)].reshape(128, 128)
        u = basis[pl.ds(8 * b, 8)].reshape(256, 128)
        cfx[1, b] = lanes_of(eighths(nt(x, u)), group_key).astype(BF16)
        return 0

    lax.fori_loop(0, 8, leaf_up, 0, unroll=8)
    ordered = nn(cfx[1, 0:8].reshape(128, 256), perm[...]).astype(BF16)
    for b in range(8):
        cfx[1, b] = ordered[16 * b : 16 * b + 16]

    tr_copy.wait()
    ttr_copy.wait()
    row, lane = iota((96, 256), 0), iota((96, 256), 1)
    above = lane - 128
    parents = ones_where(
        ((row < 64) & (lane < 127) & (row == (lane >> 1)))
        | ((row >= 64) & (above >= 0) & (above < 62) & (row - 32 == top_parent(top_place(above))))
    )
    lane = iota((8, 128), 1)
    own_mask = ones_where(iota((8, 128), 0) == (lane & 7)).astype(F32)
    top_mask = ones_where(iota((8, 128), 0) == (top_place(lane) & 7)).astype(F32)
    trf[...] = jnp.zeros_like(trf)
    ttrf[...] = jnp.zeros_like(ttrf)
    trf[:, :, 0:127] = tr[...].astype(F32)
    ttrf[:, :, 0:62] = ttr[...].astype(F32)

    def spread(ref, i, mask):
        rows = [jnp.broadcast_to(ref[i, j : j + 1, :], (8, 128)) * mask for j in range(32)]
        return jnp.concatenate(rows, axis=0).astype(BF16)

    def put(dst, at, pair, count, start):
        for g in range(count):
            both = [r[start + 8 * g : start + 8 * g + 8] for r in pair]
            dst[g, at, :] = jnp.concatenate(both, axis=0).astype(BF16)

    def transfer_rows(q, _):
        at = pl.ds(pl.multiple_of(16 * q, 16), 16)
        pair = []
        for e in range(2):
            both = [spread(trf, 2 * q + e, own_mask), spread(ttrf, 2 * q + e, top_mask)]
            pair.append(nt(parents, jnp.concatenate(both, axis=1)))
        put(w, at, pair, 8, 0)
        put(wtop, at, pair, 4, 64)
        return 0

    lax.fori_loop(0, 16, transfer_rows, 0, unroll=8)
    row, lane = iota((128, 256), 0), iota((128, 256), 1)
    root_rows = ones_where((lane & 7 == 7) & ((lane >> 3) == (row & 31)))
    wrep[...] = nn(root_rows, w[7]).astype(BF16)

    low = octet_key < 4

    def up(x0, x1, mat):
        r = nt(jnp.concatenate([x0, x1], axis=0), mat)
        return jnp.where(low, r[:16], r[16:]).astype(BF16)

    for b in range(7):
        cfx[1, 8 + b] = up(cfx[1, 2 * b], cfx[1, 2 * b + 1], w[b])
    last = jnp.zeros((16, 256), BF16)
    for _ in range(3):
        last = up(cfx[1, 14], last, w[7])
    cfx[1, 15] = last
    roots[slot] = nt(last, wrep[...]).astype(BF16)

    a_copies = [
        remote(roots.at[slot], roots.at[slot], a_send.at[k], a_recv.at[slot], a_peer(k))
        for k in range(1, 8)
    ]
    for copy in a_copies:
        copy.start()
    cf_right = remote(cfx.at[1], cfx.at[0], cf_send.at[0], cf_recv.at[0], right)
    cf_left = remote(cfx.at[1], cfx.at[2], cf_send.at[1], cf_recv.at[1], left)
    cf_right.start()
    cf_left.start()

    cp_copy.wait()
    tcp_copy.wait()
    eye = ones_where(iota((128, 127), 0) == iota((128, 127), 1))

    def coupling_rows(q, _):
        at = pl.ds(pl.multiple_of(16 * q, 16), 16)
        pair = []
        for e in range(2):
            rows = [cp[f, 2 * q + e] for f in range(6)] + [jnp.zeros((64, 127), BF16)]
            pair.append(nt(eye, jnp.concatenate(rows, axis=0)))
        put(s, at, pair, 16, 0)
        return 0

    lax.fori_loop(0, 16, coupling_rows, 0, unroll=8)

    level = (iota((48, 63), 0) >> 3) + 1
    mine = 64 - (128 >> level) + (me >> level) == iota((48, 63), 1)
    chosen = [ones_where(mine & ((iota((48, 63), 0) & 7) == e)) for e in range(8)]
    blank = jnp.zeros((32, 63), BF16)
    eights = []
    for o in range(4):
        total = None
        for e in range(8):
            i = 8 * o + e
            rows = [tcp[f, i] for f in range(6)] + [ttrf[i, :, 0:63].astype(BF16), blank]
            r = nt(chosen[e], jnp.concatenate(rows, axis=0))
            total = r if total is None else total + r
        eights.append(total)
    for h in range(6):
        stop[h] = jnp.concatenate([r[8 * h : 8 * h + 8] for r in eights], axis=0).astype(BF16)
    path = wrep[0:32, :]
    above_path[0] = path
    for h in range(5):
        padded = jnp.concatenate([jnp.zeros((64, 256), BF16), path, jnp.zeros((32, 256), BF16)], axis=0)
        path = nn(stop[h, :, 128:256], padded).astype(BF16)
        above_path[h + 1] = path

    for k in range(1, 8):
        source = (slot + 8 - k) % 8
        remote(
            roots.at[slot], roots.at[source], a_send.at[k], a_recv.at[source], a_peer(k)
        ).wait_recv()
    packed = None
    for m in (3, 2, 1, 0):
        pair = roots[2 * m].astype(F32) + roots[2 * m + 1].astype(F32)
        packed = pair if packed is None else jnp.where(group_key[:, :128] == m, pair, packed)
    topz[z] = packed.astype(BF16)
    b_copies = [
        remote(topz.at[z], topz.at[z], b_send.at[k], b_recv.at[z], b_peer(k)) for k in range(1, 8)
    ]
    for copy in b_copies:
        copy.start()

    for copy in list_copies:
        copy.wait()
    rhs_right.wait_recv()
    rhs_left.wait_recv()

    def near_leaf(k, _):
        part = [ext[near_list[f, k] & 255] for f in range(4)]
        total = None
        for h in range(2):
            x = jnp.concatenate([part[2 * h], part[2 * h + 1]], axis=1)
            v = jnp.concatenate([near_v[k, 2 * h], near_v[k, 2 * h + 1]], axis=1)
            r = nt(x, v)
            total = r if total is None else total + r
        acc[k] = total
        return 0

    for k in range(CHUNKS):
        near_copies[k].wait()
        lax.fori_loop(per * k, per * k + per, near_leaf, 0, unroll=16)

    for k in range(1, 8):
        source = (z + 8 - k) % 8
        remote(
            topz.at[z], topz.at[source], b_send.at[k], b_recv.at[source], b_peer(k)
        ).wait_recv()
    pairs = [jnp.concatenate([topz[2 * h], topz[2 * h + 1]], axis=1) for h in range(4)]
    ordered = nn(jnp.concatenate(pairs, axis=0), perm[...]).astype(BF16)
    for b in range(4):
        topc[b] = ordered[16 * b : 16 * b + 16]
    for b in range(3):
        topc[4 + b] = up(topc[2 * b], topc[2 * b + 1], wtop[b])
    last = jnp.zeros((16, 256), BF16)
    for _ in range(3):
        last = up(topc[6], last, wtop[3])
    topc[7] = last
    r = nn(topc[...].reshape(128, 256), rep[...]).astype(BF16)
    for b in range(8):
        for m in range(8):
            tope[8 * b + m] = r[16 * b : 16 * b + 16, 128 * m : 128 * m + 128]

    group = group_key[:, :128]
    nought = jnp.zeros((16, 128), BF16)

    def gathered(parts):
        lo = parts[3]
        for m in (2, 1, 0):
            lo = jnp.where(group == m, parts[m], lo)
        hi = jnp.where(group == 0, parts[4], jnp.where(group == 1, parts[5], nought))
        return jnp.concatenate([lo, hi], axis=1)

    sources = []
    for height in range(1, 7):
        node = 64 - (128 >> height) + me // (1 << height)
        parts = []
        for f in range(6):
            g = top_far[f, node] & ((64 >> height) - 1)
            if height == 1:
                place = (g & 7) * 4 + (g >> 3)
            elif height == 2:
                place = 32 + (g & 3) * 4 + (g >> 2)
            elif height == 3:
                place = 48 + (g & 1) * 4 + (g >> 1)
            else:
                place = 64 - (128 >> height) + g
            parts.append(tope[place])
        sources.append(gathered(parts))
    r = nt(jnp.concatenate(sources, axis=0), stop[...].reshape(192, 256))
    fields = r[80:96]
    key = iota((16, 192), 1) >> 5
    for h in range(5):
        fields = jnp.where(key == h, r[16 * h : 16 * h + 16], fields)
    from_above = nn(fields.astype(BF16), above_path[...].reshape(192, 256))

    cf_right.wait_recv()
    cf_left.wait_recv()
    firsts = [0, 64, 96, 112, 120, 124, 126]
    for side in range(3):
        for h in range(2):
            r = nn(cfx[side, 8 * h : 8 * h + 8].reshape(128, 256), rep[...]).astype(BF16)
            for u in range(8):
                for m in range(8):
                    node = 64 * h + 8 * u + m
                    if node == 127:
                        continue
                    lev = max(k for k in range(7) if firsts[k] <= node)
                    place = 4 * firsts[lev] + (me + side + 3) % 4 * (64 >> lev) + node - firsts[lev]
                    cfe[place] = r[16 * u : 16 * u + 16, 128 * m : 128 * m + 128]

    def couple(first_group, count, nodes_of):
        def step(b, _):
            rows = []
            for u in range(8):
                node, lev = nodes_of(b, u)
                ring = (256 >> lev) - 1
                rows.append(
                    gathered(
                        [cfe[4 * firsts[lev] + (inner_far[f, node] & ring)] for f in range(6)]
                    )
                )
            r = nt(jnp.concatenate(rows, axis=0), s[b])
            field[b] = lanes_of(eighths(r), octet_key)
            return 0

        lax.fori_loop(first_group, first_group + count, step, 0, unroll=count)

    def uniform(lev):
        return lambda b, u: (8 * b + u, lev)

    def mixed(b, u):
        node = min(120 + u, 126)
        return node, max(k for k in range(7) if firsts[k] <= node)

    couple(0, 8, uniform(0))
    couple(8, 4, uniform(1))
    couple(12, 2, uniform(2))
    couple(14, 1, uniform(3))
    couple(15, 1, mixed)

    def down(x, mat):
        lower = jnp.where(low, x, 0.0).astype(BF16)
        upper = jnp.where(low, 0.0, x).astype(BF16)
        r = nn(jnp.concatenate([lower, upper], axis=0), mat)
        return r[:16], r[16:]

    base = jnp.where(octet_key == 7, 0.0, field[15]) + from_above
    here = base
    for _ in range(2):
        here = base + down(here, w[7])[1]
    field[14] = field[14] + down(here, w[7])[0]
    for b in range(6, -1, -1):
        r0, r1 = down(field[8 + b], w[b])
        field[2 * b] = field[2 * b] + r0
        field[2 * b + 1] = field[2 * b + 1] + r1
    ordered = nt(field[0:8].reshape(128, 256).astype(BF16), perm[...])

    for b in range(8):
        x = ordered[16 * b : 16 * b + 16]
        rows = [jnp.where(group_key == m, x, 0.0).astype(BF16) for m in range(8)]
        r = nn(jnp.concatenate(rows, axis=0), basis[8 * b : 8 * b + 8].reshape(256, 128))
        for m in range(8):
            k = 8 * b + m
            out[:, 128 * k : 128 * k + 128] = (r[16 * m : 16 * m + 16] + acc[k]).astype(BF16)

    rhs_right.wait_send()
    rhs_left.wait_send()
    cf_right.wait_send()
    cf_left.wait_send()
    for copy in a_copies + b_copies:
        copy.wait_send()


def body(
    rhs_cols,
    near_blocks,
    near_list,
    leaf_basis,
    inner_transfer,
    inner_coupling,
    inner_far,
    top_transfer,
    top_coupling,
    top_far,
):
    hbm = pl.BlockSpec(memory_space=pl.ANY)
    vmem = pltpu.VMEM
    dma = pltpu.SemaphoreType.DMA
    return pl.pallas_call(
        kernel,
        out_shape=pltpu.VMEM((16, 8192), BF16),
        in_specs=[hbm] * 10,
        out_specs=pl.BlockSpec(memory_space=vmem),
        scratch_shapes=[
            vmem((16, 8192), BF16),
            pltpu.SMEM((4, 64), I32),
            pltpu.SMEM((6, 127), I32),
            pltpu.SMEM((6, 63), I32),
            vmem((64, 4, 128, 128), BF16),
            vmem((64, 32, 128), BF16),
            vmem((32, 32, 127), BF16),
            vmem((6, 32, 32, 127), BF16),
            vmem((32, 32, 62), BF16),
            vmem((6, 32, 32, 63), BF16),
            vmem((32, 32, 128), F32),
            vmem((32, 32, 128), F32),
            vmem((256, 16, 128), BF16),
            vmem((64, 16, 128), F32),
            vmem((8, 256, 256), BF16),
            vmem((4, 256, 256), BF16),
            vmem((128, 256), BF16),
            vmem((16, 256, 256), BF16),
            vmem((6, 32, 256), BF16),
            vmem((6, 32, 256), BF16),
            vmem((256, 256), BF16),
            vmem((256, 1024), BF16),
            vmem((3, 16, 16, 256), BF16),
            vmem((512, 16, 128), BF16),
            vmem((16, 16, 256), F32),
            vmem((8, 16, 128), BF16),
            vmem((8, 16, 128), BF16),
            vmem((8, 16, 256), BF16),
            vmem((64, 16, 128), BF16),
            dma((9 + CHUNKS,)),
            dma((2,)),
            dma((2,)),
            dma((2,)),
            dma((2,)),
            dma((8,)),
            dma((8,)),
            dma((8,)),
            dma((8,)),
        ],
        compiler_params=pltpu.CompilerParams(
            collective_id=0, has_side_effects=True, vmem_limit_bytes=56 * 1024 * 1024
        ),
        name="h2_product",
    )(
        near_list.T,
        inner_far.T,
        top_far.T,
        rhs_cols,
        near_blocks,
        leaf_basis,
        inner_transfer.transpose(1, 2, 0),
        inner_coupling.transpose(1, 2, 3, 0),
        top_transfer.transpose(1, 2, 0),
        top_coupling.transpose(1, 2, 3, 0),
    )


def solution(mesh):
    return jax.shard_map(
        body,
        mesh=mesh,
        in_specs=(
            P("rhs", "leaf"),
            P("leaf", None, None, None),
            P("leaf", None),
            P("leaf", None, None),
            P("leaf", None, None),
            P("leaf", None, None, None),
            P("leaf", None),
            P(),
            P(),
            P(),
        ),
        out_specs=P("rhs", "leaf"),
        check_vma=False,
    )
```

```python
import functools

import jax
import jax.numpy as jnp
from jax import lax
from jax.experimental import pallas as pl
from jax.experimental.pallas import tpu as pltpu
from jax.sharding import PartitionSpec as P

MESH = pl.DeviceIdType.MESH
F32 = jnp.float32
BF16 = jnp.bfloat16
I32 = jnp.int32
CHUNKS = 4


def nt(a, b):
    return lax.dot_general(a, b, (((1,), (1,)), ((), ())), preferred_element_type=F32)


def nn(a, b):
    return lax.dot_general(a, b, (((1,), (0,)), ((), ())), preferred_element_type=F32)


def iota(shape, dim):
    return lax.broadcasted_iota(I32, shape, dim)


def ones_where(cond):
    return jnp.where(cond, 1.0, 0.0).astype(BF16)


def lanes_of(rows, key):
    out = rows[7]
    for m in range(7):
        out = jnp.where(key == m, rows[m], out)
    return out


def eighths(r):
    return [r[16 * m : 16 * m + 16] for m in range(8)]


def top_place(t):
    return jnp.where(
        t < 32,
        (t & 7) * 4 + (t >> 3),
        jnp.where(
            t < 48,
            32 + (t & 3) * 4 + ((t - 32) >> 2),
            jnp.where(t < 56, 48 + (t & 1) * 4 + ((t - 48) >> 1), t),
        ),
    )


def top_parent(place):
    return jnp.where(
        place < 56,
        32 + (place >> 3) * 4 + (place & 3),
        jnp.where(place < 60, 60 + ((place - 56) >> 1), 62),
    )


def kernel(
    near_list_in,
    inner_far_in,
    top_far_in,
    rhs,
    near,
    basis_in,
    tr_in,
    cp_in,
    ttr_in,
    tcp_in,
    out,
    rhs_v,
    near_list,
    inner_far,
    top_far,
    near_v,
    basis,
    tr,
    cp,
    ttr,
    tcp,
    trf,
    ttrf,
    ext,
    acc,
    w,
    wtop,
    wrep,
    s,
    stop,
    above_path,
    perm,
    rep,
    cfx,
    cfe,
    field,
    roots,
    topz,
    topc,
    tope,
    loc,
    rhs_send,
    rhs_recv,
    cf_send,
    cf_recv,
    a_send,
    a_recv,
    b_send,
    b_recv,
):
    me = lax.axis_index("leaf")
    col = lax.axis_index("rhs")
    core = me % 2
    z = (me // 2) % 8
    y = me // 16
    slot = y * 2 + core

    def local(src, dst, k):
        copy = pltpu.make_async_copy(src, dst, loc.at[k])
        copy.start()
        return copy

    rhs_copy = local(rhs, rhs_v, 0)
    basis_copy = local(basis_in, basis, 1)
    tr_copy = local(tr_in, tr, 2)
    ttr_copy = local(ttr_in, ttr, 3)
    cp_copy = local(cp_in, cp, 4)
    tcp_copy = local(tcp_in, tcp, 5)
    list_copies = [
        local(near_list_in, near_list, 6 + CHUNKS),
        local(inner_far_in, inner_far, 7 + CHUNKS),
        local(top_far_in, top_far, 8 + CHUNKS),
    ]
    per = 64 // CHUNKS
    near_copies = [
        local(near.at[pl.ds(per * k, per)], near_v.at[pl.ds(per * k, per)], 6 + k)
        for k in range(CHUNKS)
    ]

    right = (me + 1) % 64
    left = (me + 63) % 64

    def a_peer(k):
        other = (slot + k) % 8
        return ((other // 2) * 8 + z) * 2 + other % 2

    def b_peer(k):
        return (y * 8 + (z + k) % 8) * 2 + core

    barrier = pltpu.get_barrier_semaphore()
    for peer in [right, left] + [a_peer(k) for k in range(1, 8)] + [b_peer(k) for k in range(1, 8)]:
        pl.semaphore_signal(barrier, inc=1, device_id=(peer, col), device_id_type=MESH)

    row, lane = iota((256, 256), 0), iota((256, 256), 1)
    perm[...] = ones_where(((row >> 5) == (lane & 7)) & ((row & 31) == (lane >> 3)))
    lane = iota((16, 256), 1)
    octet_key = lane & 7
    group_key = lane >> 5

    own = (me % 4) * 64
    rhs_copy.wait()
    for k in range(64):
        ext[own + k] = rhs_v[:, 128 * k : 128 * k + 128]

    def remote(src, dst, send, recv, peer):
        return pltpu.make_async_remote_copy(
            src_ref=src,
            dst_ref=dst,
            send_sem=send,
            recv_sem=recv,
            device_id=(peer, col),
            device_id_type=MESH,
        )

    mine = ext.at[pl.ds(own, 64)]
    rhs_right = remote(mine, mine, rhs_send.at[0], rhs_recv.at[0], right)
    rhs_left = remote(mine, mine, rhs_send.at[1], rhs_recv.at[1], left)

    basis_copy.wait()

    def leaf_up(b, _):
        x = ext[pl.ds(own + 8 * b, 8)].reshape(128, 128)
        u = basis[pl.ds(8 * b, 8)].reshape(256, 128)
        cfx[1, b] = lanes_of(eighths(nt(x, u)), group_key).astype(BF16)
        return 0

    lax.fori_loop(0, 8, leaf_up, 0, unroll=8)
    ordered = nn(cfx[1, 0:8].reshape(128, 256), perm[...]).astype(BF16)
    for b in range(8):
        cfx[1, b] = ordered[16 * b : 16 * b + 16]

    tr_copy.wait()
    lane = iota((64, 128), 1)
    own_parent = ones_where((iota((64, 128), 0) == (lane >> 1)) & (lane < 127))
    lane = iota((8, 128), 1)
    own_mask = ones_where(iota((8, 128), 0) == (lane & 7)).astype(F32)
    trf[...] = jnp.zeros_like(trf)
    trf[:, :, 0:127] = tr[...].astype(F32)

    def spread(ref, i, mask):
        rows = [jnp.broadcast_to(ref[i, j : j + 1, :], (8, 128)) * mask for j in range(32)]
        return jnp.concatenate(rows, axis=0).astype(BF16)

    def put(dst, at, pair, count, start):
        for g in range(count):
            both = [r[start + 8 * g : start + 8 * g + 8] for r in pair]
            dst[g, at, :] = jnp.concatenate(both, axis=0).astype(BF16)

    def transfer_rows(q, _):
        at = pl.ds(pl.multiple_of(16 * q, 16), 16)
        put(w, at, [nt(own_parent, spread(trf, 2 * q + e, own_mask)) for e in range(2)], 8, 0)
        return 0

    lax.fori_loop(0, 16, transfer_rows, 0, unroll=8)
    row, lane = iota((128, 256), 0), iota((128, 256), 1)
    root_rows = ones_where((lane & 7 == 7) & ((lane >> 3) == (row & 31)))
    wrep[...] = nn(root_rows, w[7]).astype(BF16)

    low = octet_key < 4

    def up(x0, x1, mat):
        r = nt(jnp.concatenate([x0, x1], axis=0), mat)
        return jnp.where(low, r[:16], r[16:]).astype(BF16)

    for b in range(7):
        cfx[1, 8 + b] = up(cfx[1, 2 * b], cfx[1, 2 * b + 1], w[b])
    last = jnp.zeros((16, 256), BF16)
    for _ in range(3):
        last = up(cfx[1, 14], last, w[7])
    cfx[1, 15] = last
    roots[slot] = nt(last, wrep[...]).astype(BF16)

    a_copies = [
        remote(roots.at[slot], roots.at[slot], a_send.at[k], a_recv.at[slot], a_peer(k))
        for k in range(1, 8)
    ]
    pl.semaphore_wait(barrier, 16)
    for copy in a_copies:
        copy.start()
    rhs_right.start()
    rhs_left.start()
    cf_right = remote(cfx.at[1], cfx.at[0], cf_send.at[0], cf_recv.at[0], right)
    cf_left = remote(cfx.at[1], cfx.at[2], cf_send.at[1], cf_recv.at[1], left)
    cf_right.start()
    cf_left.start()

    row, lane = iota((256, 1024), 0), iota((256, 1024), 1)
    rep[...] = ones_where(((row >> 3) == (lane & 31)) & ((row & 7) == (lane >> 7)))

    cp_copy.wait()
    tcp_copy.wait()
    ttr_copy.wait()
    ttrf[...] = jnp.zeros_like(ttrf)
    ttrf[:, :, 0:62] = ttr[...].astype(F32)
    top_mask = ones_where(iota((8, 128), 0) == (top_place(iota((8, 128), 1)) & 7)).astype(F32)
    row, lane = iota((160, 255), 0), iota((160, 255), 1)
    parent = top_parent(top_place(lane))
    picks = ones_where(
        ((row < 128) & (lane - 128 == row))
        | ((row >= 128) & (lane < 62) & (row - 96 == parent))
    )

    def coupling_rows(q, _):
        at = pl.ds(pl.multiple_of(16 * q, 16), 16)
        pair = []
        for e in range(2):
            rows = [cp[f, 2 * q + e] for f in range(6)] + [jnp.zeros((64, 127), BF16)]
            both = [spread(ttrf, 2 * q + e, top_mask), jnp.concatenate(rows, axis=0)]
            pair.append(nt(picks, jnp.concatenate(both, axis=1)))
        put(s, at, pair, 16, 0)
        put(wtop, at, pair, 4, 128)
        return 0

    lax.fori_loop(0, 16, coupling_rows, 0, unroll=8)

    level = (iota((48, 63), 0) >> 3) + 1
    mine = 64 - (128 >> level) + (me >> level) == iota((48, 63), 1)
    chosen = [ones_where(mine & ((iota((48, 63), 0) & 7) == e)) for e in range(8)]
    blank = jnp.zeros((32, 63), BF16)
    eights = []
    for o in range(4):
        total = None
        for e in range(8):
            i = 8 * o + e
            rows = [tcp[f, i] for f in range(6)] + [ttrf[i, :, 0:63].astype(BF16), blank]
            r = nt(chosen[e], jnp.concatenate(rows, axis=0))
            total = r if total is None else total + r
        eights.append(total)
    for h in range(6):
        stop[h] = jnp.concatenate([r[8 * h : 8 * h + 8] for r in eights], axis=0).astype(BF16)
    path = wrep[0:32, :]
    above_path[0] = path
    for h in range(5):
        padded = jnp.concatenate([jnp.zeros((64, 256), BF16), path, jnp.zeros((32, 256), BF16)], axis=0)
        path = nn(stop[h, :, 128:256], padded).astype(BF16)
        above_path[h + 1] = path

    group = group_key[:, :128]
    nought = jnp.zeros((16, 128), BF16)

    def gathered(parts):
        lo = parts[3]
        for m in (2, 1, 0):
            lo = jnp.where(group == m, parts[m], lo)
        hi = jnp.where(group == 0, parts[4], jnp.where(group == 1, parts[5], nought))
        return jnp.concatenate([lo, hi], axis=1)

    for copy in list_copies:
        copy.wait()
    rhs_right.wait_recv()
    rhs_left.wait_recv()

    def near_leaf(k, _):
        part = [ext[near_list[f, k] & 255] for f in range(4)]
        total = None
        for h in range(2):
            x = jnp.concatenate([part[2 * h], part[2 * h + 1]], axis=1)
            v = jnp.concatenate([near_v[k, 2 * h], near_v[k, 2 * h + 1]], axis=1)
            r = nt(x, v)
            total = r if total is None else total + r
        acc[k] = total
        return 0

    for k in range(1, 8):
        source = (slot + 8 - k) % 8
        remote(
            roots.at[slot], roots.at[source], a_send.at[k], a_recv.at[source], a_peer(k)
        ).wait_recv()
    packed = None
    for m in (3, 2, 1, 0):
        pair = roots[2 * m].astype(F32) + roots[2 * m + 1].astype(F32)
        packed = pair if packed is None else jnp.where(group_key[:, :128] == m, pair, packed)
    topz[z] = packed.astype(BF16)
    b_copies = [
        remote(topz.at[z], topz.at[z], b_send.at[k], b_recv.at[z], b_peer(k)) for k in range(1, 8)
    ]
    for copy in b_copies:
        copy.start()

    for k in range(0, 4):
        near_copies[k].wait()
        lax.fori_loop(per * k, per * k + per, near_leaf, 0, unroll=16)

    cf_right.wait_recv()
    cf_left.wait_recv()
    firsts = [0, 64, 96, 112, 120, 124, 126]
    for side in range(3):
        for h in range(2):
            r = nn(cfx[side, 8 * h : 8 * h + 8].reshape(128, 256), rep[...]).astype(BF16)
            for u in range(8):
                for m in range(8):
                    node = 64 * h + 8 * u + m
                    if node == 127:
                        continue
                    lev = max(k for k in range(7) if firsts[k] <= node)
                    place = 4 * firsts[lev] + (me + side + 3) % 4 * (64 >> lev) + node - firsts[lev]
                    cfe[place] = r[16 * u : 16 * u + 16, 128 * m : 128 * m + 128]

    def couple(first_group, count, nodes_of):
        def step(b, _):
            rows = []
            for u in range(8):
                node, lev = nodes_of(b, u)
                ring = (256 >> lev) - 1
                rows.append(
                    gathered(
                        [cfe[4 * firsts[lev] + (inner_far[f, node] & ring)] for f in range(6)]
                    )
                )
            r = nt(jnp.concatenate(rows, axis=0), s[b])
            field[b] = lanes_of(eighths(r), octet_key)
            return 0

        lax.fori_loop(first_group, first_group + count, step, 0, unroll=count)

    def uniform(lev):
        return lambda b, u: (8 * b + u, lev)

    def mixed(b, u):
        node = min(120 + u, 126)
        return node, max(k for k in range(7) if firsts[k] <= node)

    couple(0, 8, uniform(0))
    couple(8, 4, uniform(1))
    couple(12, 2, uniform(2))
    couple(14, 1, uniform(3))
    couple(15, 1, mixed)

    for k in range(1, 8):
        source = (z + 8 - k) % 8
        remote(
            topz.at[z], topz.at[source], b_send.at[k], b_recv.at[source], b_peer(k)
        ).wait_recv()
    pairs = [jnp.concatenate([topz[2 * h], topz[2 * h + 1]], axis=1) for h in range(4)]
    ordered = nn(jnp.concatenate(pairs, axis=0), perm[...]).astype(BF16)
    for b in range(4):
        topc[b] = ordered[16 * b : 16 * b + 16]
    for b in range(3):
        topc[4 + b] = up(topc[2 * b], topc[2 * b + 1], wtop[b])
    last = jnp.zeros((16, 256), BF16)
    for _ in range(3):
        last = up(topc[6], last, wtop[3])
    topc[7] = last
    r = nn(topc[...].reshape(128, 256), rep[...]).astype(BF16)
    for b in range(8):
        for m in range(8):
            tope[8 * b + m] = r[16 * b : 16 * b + 16, 128 * m : 128 * m + 128]

    sources = []
    for height in range(1, 7):
        node = 64 - (128 >> height) + me // (1 << height)
        parts = []
        for f in range(6):
            g = top_far[f, node] & ((64 >> height) - 1)
            if height == 1:
                place = (g & 7) * 4 + (g >> 3)
            elif height == 2:
                place = 32 + (g & 3) * 4 + (g >> 2)
            elif height == 3:
                place = 48 + (g & 1) * 4 + (g >> 1)
            else:
                place = 64 - (128 >> height) + g
            parts.append(tope[place])
        sources.append(gathered(parts))
    r = nt(jnp.concatenate(sources, axis=0), stop[...].reshape(192, 256))
    fields = r[80:96]
    key = iota((16, 192), 1) >> 5
    for h in range(5):
        fields = jnp.where(key == h, r[16 * h : 16 * h + 16], fields)
    from_above = nn(fields.astype(BF16), above_path[...].reshape(192, 256))

    def down(x, mat):
        lower = jnp.where(low, x, 0.0).astype(BF16)
        upper = jnp.where(low, 0.0, x).astype(BF16)
        r = nn(jnp.concatenate([lower, upper], axis=0), mat)
        return r[:16], r[16:]

    base = jnp.where(octet_key == 7, 0.0, field[15]) + from_above
    here = base
    for _ in range(2):
        here = base + down(here, w[7])[1]
    field[14] = field[14] + down(here, w[7])[0]
    for b in range(6, -1, -1):
        r0, r1 = down(field[8 + b], w[b])
        field[2 * b] = field[2 * b] + r0
        field[2 * b + 1] = field[2 * b + 1] + r1
    ordered = nt(field[0:8].reshape(128, 256).astype(BF16), perm[...])

    for b in range(8):
        x = ordered[16 * b : 16 * b + 16]
        rows = [jnp.where(group_key == m, x, 0.0).astype(BF16) for m in range(8)]
        r = nn(jnp.concatenate(rows, axis=0), basis[8 * b : 8 * b + 8].reshape(256, 128))
        for m in range(8):
            k = 8 * b + m
            out[:, 128 * k : 128 * k + 128] = (r[16 * m : 16 * m + 16] + acc[k]).astype(BF16)

    rhs_right.wait_send()
    rhs_left.wait_send()
    cf_right.wait_send()
    cf_left.wait_send()
    for copy in a_copies + b_copies:
        copy.wait_send()


def body(
    rhs_cols,
    near_blocks,
    near_list,
    leaf_basis,
    inner_transfer,
    inner_coupling,
    inner_far,
    top_transfer,
    top_coupling,
    top_far,
):
    hbm = pl.BlockSpec(memory_space=pl.ANY)
    vmem = pltpu.VMEM
    dma = pltpu.SemaphoreType.DMA
    return pl.pallas_call(
        kernel,
        out_shape=pltpu.VMEM((16, 8192), BF16),
        in_specs=[hbm] * 10,
        out_specs=pl.BlockSpec(memory_space=vmem),
        scratch_shapes=[
            vmem((16, 8192), BF16),
            pltpu.SMEM((4, 64), I32),
            pltpu.SMEM((6, 127), I32),
            pltpu.SMEM((6, 63), I32),
            vmem((64, 4, 128, 128), BF16),
            vmem((64, 32, 128), BF16),
            vmem((32, 32, 127), BF16),
            vmem((6, 32, 32, 127), BF16),
            vmem((32, 32, 62), BF16),
            vmem((6, 32, 32, 63), BF16),
            vmem((32, 32, 128), F32),
            vmem((32, 32, 128), F32),
            vmem((256, 16, 128), BF16),
            vmem((64, 16, 128), F32),
            vmem((8, 256, 256), BF16),
            vmem((4, 256, 256), BF16),
            vmem((128, 256), BF16),
            vmem((16, 256, 256), BF16),
            vmem((6, 32, 256), BF16),
            vmem((6, 32, 256), BF16),
            vmem((256, 256), BF16),
            vmem((256, 1024), BF16),
            vmem((3, 16, 16, 256), BF16),
            vmem((512, 16, 128), BF16),
            vmem((16, 16, 256), F32),
            vmem((8, 16, 128), BF16),
            vmem((8, 16, 128), BF16),
            vmem((8, 16, 256), BF16),
            vmem((64, 16, 128), BF16),
            dma((9 + CHUNKS,)),
            dma((2,)),
            dma((2,)),
            dma((2,)),
            dma((2,)),
            dma((8,)),
            dma((8,)),
            dma((8,)),
            dma((8,)),
        ],
        compiler_params=pltpu.CompilerParams(
            collective_id=0, has_side_effects=True, vmem_limit_bytes=56 * 1024 * 1024
        ),
        name="h2_product",
    )(
        near_list.T,
        inner_far.T,
        top_far.T,
        rhs_cols,
        near_blocks,
        leaf_basis,
        inner_transfer.transpose(1, 2, 0),
        inner_coupling.transpose(1, 2, 3, 0),
        top_transfer.transpose(1, 2, 0),
        top_coupling.transpose(1, 2, 3, 0),
    )


def solution(mesh):
    return jax.shard_map(
        body,
        mesh=mesh,
        in_specs=(
            P("rhs", "leaf"),
            P("leaf", None, None, None),
            P("leaf", None),
            P("leaf", None, None),
            P("leaf", None, None),
            P("leaf", None, None, None),
            P("leaf", None),
            P(),
            P(),
            P(),
        ),
        out_specs=P("rhs", "leaf"),
        check_vma=False,
    )
```

```python
import functools

import jax
import jax.numpy as jnp
from jax import lax
from jax.experimental import pallas as pl
from jax.experimental.pallas import tpu as pltpu
from jax.sharding import PartitionSpec as P

MESH = pl.DeviceIdType.MESH
F32 = jnp.float32
BF16 = jnp.bfloat16
I32 = jnp.int32
CHUNKS = 2


def nt(a, b):
    return lax.dot_general(a, b, (((1,), (1,)), ((), ())), preferred_element_type=F32)


def nn(a, b):
    return lax.dot_general(a, b, (((1,), (0,)), ((), ())), preferred_element_type=F32)


def iota(shape, dim):
    return lax.broadcasted_iota(I32, shape, dim)


def ones_where(cond):
    return jnp.where(cond, 1.0, 0.0).astype(BF16)


def lanes_of(rows, key):
    out = rows[7]
    for m in range(7):
        out = jnp.where(key == m, rows[m], out)
    return out


def eighths(r):
    return [r[16 * m : 16 * m + 16] for m in range(8)]


def top_place(t):
    return jnp.where(
        t < 32,
        (t & 7) * 4 + (t >> 3),
        jnp.where(
            t < 48,
            32 + (t & 3) * 4 + ((t - 32) >> 2),
            jnp.where(t < 56, 48 + (t & 1) * 4 + ((t - 48) >> 1), t),
        ),
    )


def top_parent(place):
    return jnp.where(
        place < 56,
        32 + (place >> 3) * 4 + (place & 3),
        jnp.where(place < 60, 60 + ((place - 56) >> 1), 62),
    )


def kernel(
    near_list_in,
    inner_far_in,
    top_far_in,
    rhs,
    near,
    basis_in,
    tr_in,
    cp_in,
    ttr_in,
    tcp_in,
    out,
    rhs_v,
    near_list,
    inner_far,
    top_far,
    near_v,
    basis,
    tr,
    cp,
    ttr,
    tcp,
    trf,
    ttrf,
    ext,
    acc,
    w,
    wtop,
    wrep,
    s,
    stop,
    above_path,
    perm,
    rep,
    cfx,
    cfe,
    field,
    roots,
    topz,
    topc,
    tope,
    loc,
    rhs_send,
    rhs_recv,
    cf_send,
    cf_recv,
    a_send,
    a_recv,
    b_send,
    b_recv,
):
    me = lax.axis_index("leaf")
    col = lax.axis_index("rhs")
    core = me % 2
    z = (me // 2) % 8
    y = me // 16
    slot = y * 2 + core

    def local(src, dst, k):
        copy = pltpu.make_async_copy(src, dst, loc.at[k])
        copy.start()
        return copy

    rhs_copy = local(rhs, rhs_v, 0)
    basis_copy = local(basis_in, basis, 1)
    tr_copy = local(tr_in, tr, 2)
    ttr_copy = local(ttr_in, ttr, 3)
    cp_copy = local(cp_in, cp, 4)
    tcp_copy = local(tcp_in, tcp, 5)
    list_copies = [
        local(near_list_in, near_list, 6 + CHUNKS),
        local(inner_far_in, inner_far, 7 + CHUNKS),
        local(top_far_in, top_far, 8 + CHUNKS),
    ]
    per = 64 // CHUNKS
    near_copies = [
        local(near.at[pl.ds(per * k, per)], near_v.at[pl.ds(per * k, per)], 6 + k)
        for k in range(CHUNKS)
    ]

    right = (me + 1) % 64
    left = (me + 63) % 64

    def a_peer(k):
        other = (slot + k) % 8
        return ((other // 2) * 8 + z) * 2 + other % 2

    def b_peer(k):
        return (y * 8 + (z + k) % 8) * 2 + core

    barrier = pltpu.get_barrier_semaphore()
    for peer in [right, left] + [a_peer(k) for k in range(1, 8)] + [b_peer(k) for k in range(1, 8)]:
        pl.semaphore_signal(barrier, inc=1, device_id=(peer, col), device_id_type=MESH)

    row, lane = iota((256, 256), 0), iota((256, 256), 1)
    perm[...] = ones_where(((row >> 5) == (lane & 7)) & ((row & 31) == (lane >> 3)))
    lane = iota((16, 256), 1)
    octet_key = lane & 7
    group_key = lane >> 5

    own = (me % 4) * 64
    rhs_copy.wait()
    for k in range(64):
        ext[own + k] = rhs_v[:, 128 * k : 128 * k + 128]

    def remote(src, dst, send, recv, peer):
        return pltpu.make_async_remote_copy(
            src_ref=src,
            dst_ref=dst,
            send_sem=send,
            recv_sem=recv,
            device_id=(peer, col),
            device_id_type=MESH,
        )

    mine = ext.at[pl.ds(own, 64)]
    rhs_right = remote(mine, mine, rhs_send.at[0], rhs_recv.at[0], right)
    rhs_left = remote(mine, mine, rhs_send.at[1], rhs_recv.at[1], left)

    basis_copy.wait()

    def leaf_up(b, _):
        x = ext[pl.ds(own + 8 * b, 8)].reshape(128, 128)
        u = basis[pl.ds(8 * b, 8)].reshape(256, 128)
        cfx[1, b] = lanes_of(eighths(nt(x, u)), group_key).astype(BF16)
        return 0

    lax.fori_loop(0, 8, leaf_up, 0, unroll=8)
    ordered = nn(cfx[1, 0:8].reshape(128, 256), perm[...]).astype(BF16)
    for b in range(8):
        cfx[1, b] = ordered[16 * b : 16 * b + 16]

    tr_copy.wait()
    lane = iota((64, 128), 1)
    own_parent = ones_where((iota((64, 128), 0) == (lane >> 1)) & (lane < 127))
    lane = iota((8, 128), 1)
    own_mask = ones_where(iota((8, 128), 0) == (lane & 7)).astype(F32)
    trf[...] = jnp.zeros_like(trf)
    trf[:, :, 0:127] = tr[...].astype(F32)

    def spread(ref, i, mask):
        rows = [jnp.broadcast_to(ref[i, j : j + 1, :], (8, 128)) * mask for j in range(32)]
        return jnp.concatenate(rows, axis=0).astype(BF16)

    def put(dst, at, pair, count, start):
        for g in range(count):
            both = [r[start + 8 * g : start + 8 * g + 8] for r in pair]
            dst[g, at, :] = jnp.concatenate(both, axis=0).astype(BF16)

    def transfer_rows(q, _):
        at = pl.ds(pl.multiple_of(16 * q, 16), 16)
        put(w, at, [nt(own_parent, spread(trf, 2 * q + e, own_mask)) for e in range(2)], 8, 0)
        return 0

    lax.fori_loop(0, 16, transfer_rows, 0, unroll=16)
    row, lane = iota((128, 256), 0), iota((128, 256), 1)
    root_rows = ones_where((lane & 7 == 7) & ((lane >> 3) == (row & 31)))
    wrep[...] = nn(root_rows, w[7]).astype(BF16)

    low = octet_key < 4

    def up(x0, x1, mat):
        r = nt(jnp.concatenate([x0, x1], axis=0), mat)
        return jnp.where(low, r[:16], r[16:]).astype(BF16)

    for b in range(7):
        cfx[1, 8 + b] = up(cfx[1, 2 * b], cfx[1, 2 * b + 1], w[b])
    last = jnp.zeros((16, 256), BF16)
    for _ in range(3):
        last = up(cfx[1, 14], last, w[7])
    cfx[1, 15] = last
    roots[slot] = nt(last, wrep[...]).astype(BF16)

    a_copies = [
        remote(roots.at[slot], roots.at[slot], a_send.at[k], a_recv.at[slot], a_peer(k))
        for k in range(1, 8)
    ]
    pl.semaphore_wait(barrier, 16)
    for copy in a_copies:
        copy.start()
    rhs_right.start()
    rhs_left.start()
    cf_right = remote(cfx.at[1], cfx.at[0], cf_send.at[0], cf_recv.at[0], right)
    cf_left = remote(cfx.at[1], cfx.at[2], cf_send.at[1], cf_recv.at[1], left)
    cf_right.start()
    cf_left.start()

    row, lane = iota((256, 1024), 0), iota((256, 1024), 1)
    rep[...] = ones_where(((row >> 3) == (lane & 31)) & ((row & 7) == (lane >> 7)))

    cp_copy.wait()
    tcp_copy.wait()
    ttr_copy.wait()
    ttrf[...] = jnp.zeros_like(ttrf)
    ttrf[:, :, 0:62] = ttr[...].astype(F32)
    top_mask = ones_where(iota((8, 128), 0) == (top_place(iota((8, 128), 1)) & 7)).astype(F32)
    lane = iota((32, 128), 1)
    top_picks = ones_where((lane < 62) & (iota((32, 128), 0) + 32 == top_parent(top_place(lane))))

    def coupling_rows(q, _):
        at = pl.ds(pl.multiple_of(16 * q, 16), 16)
        pair = []
        for e in range(2):
            rows = [cp[f, 2 * q + e] for f in range(6)]
            turned = jnp.transpose(jnp.concatenate(rows, axis=0).astype(F32))
            turned = jnp.concatenate([turned, jnp.zeros((1, 192), F32)], axis=0)
            pair.append(jnp.concatenate([turned, jnp.zeros((128, 64), F32)], axis=1))
        put(s, at, pair, 16, 0)
        put(wtop, at, [nt(top_picks, spread(ttrf, 2 * q + e, top_mask)) for e in range(2)], 4, 0)
        return 0

    lax.fori_loop(0, 16, coupling_rows, 0, unroll=16)

    level = (iota((48, 63), 0) >> 3) + 1
    mine = 64 - (128 >> level) + (me >> level) == iota((48, 63), 1)
    chosen = [ones_where(mine & ((iota((48, 63), 0) & 7) == e)) for e in range(8)]
    blank = jnp.zeros((32, 63), BF16)
    eights = []
    for o in range(4):
        total = None
        for e in range(8):
            i = 8 * o + e
            rows = [tcp[f, i] for f in range(6)] + [ttrf[i, :, 0:63].astype(BF16), blank]
            r = nt(chosen[e], jnp.concatenate(rows, axis=0))
            total = r if total is None else total + r
        eights.append(total)
    for h in range(6):
        stop[h] = jnp.concatenate([r[8 * h : 8 * h + 8] for r in eights], axis=0).astype(BF16)
    path = wrep[0:32, :]
    above_path[0] = path
    for h in range(5):
        padded = jnp.concatenate([jnp.zeros((64, 256), BF16), path, jnp.zeros((32, 256), BF16)], axis=0)
        path = nn(stop[h, :, 128:256], padded).astype(BF16)
        above_path[h + 1] = path

    group = group_key[:, :128]
    nought = jnp.zeros((16, 128), BF16)

    def gathered(parts):
        lo = parts[3]
        for m in (2, 1, 0):
            lo = jnp.where(group == m, parts[m], lo)
        hi = jnp.where(group == 0, parts[4], jnp.where(group == 1, parts[5], nought))
        return jnp.concatenate([lo, hi], axis=1)

    for copy in list_copies:
        copy.wait()
    rhs_right.wait_recv()
    rhs_left.wait_recv()

    def near_leaf(k, _):
        part = [ext[near_list[f, k] & 255] for f in range(4)]
        total = None
        for h in range(2):
            x = jnp.concatenate([part[2 * h], part[2 * h + 1]], axis=1)
            v = jnp.concatenate([near_v[k, 2 * h], near_v[k, 2 * h + 1]], axis=1)
            r = nt(x, v)
            total = r if total is None else total + r
        acc[k] = total
        return 0

    for k in range(1, 8):
        source = (slot + 8 - k) % 8
        remote(
            roots.at[slot], roots.at[source], a_send.at[k], a_recv.at[source], a_peer(k)
        ).wait_recv()
    packed = None
    for m in (3, 2, 1, 0):
        pair = roots[2 * m].astype(F32) + roots[2 * m + 1].astype(F32)
        packed = pair if packed is None else jnp.where(group_key[:, :128] == m, pair, packed)
    topz[z] = packed.astype(BF16)
    b_copies = [
        remote(topz.at[z], topz.at[z], b_send.at[k], b_recv.at[z], b_peer(k)) for k in range(1, 8)
    ]
    for copy in b_copies:
        copy.start()

    for k in range(0, 2):
        near_copies[k].wait()
        lax.fori_loop(per * k, per * k + per, near_leaf, 0, unroll=32)

    cf_right.wait_recv()
    cf_left.wait_recv()
    firsts = [0, 64, 96, 112, 120, 124, 126]
    for side in range(3):
        for h in range(2):
            r = nn(cfx[side, 8 * h : 8 * h + 8].reshape(128, 256), rep[...]).astype(BF16)
            for u in range(8):
                for m in range(8):
                    node = 64 * h + 8 * u + m
                    if node == 127:
                        continue
                    lev = max(k for k in range(7) if firsts[k] <= node)
                    place = 4 * firsts[lev] + (me + side + 3) % 4 * (64 >> lev) + node - firsts[lev]
                    cfe[place] = r[16 * u : 16 * u + 16, 128 * m : 128 * m + 128]

    def couple(first_group, count, nodes_of):
        def step(b, _):
            rows = []
            for u in range(8):
                node, lev = nodes_of(b, u)
                ring = (256 >> lev) - 1
                rows.append(
                    gathered(
                        [cfe[4 * firsts[lev] + (inner_far[f, node] & ring)] for f in range(6)]
                    )
                )
            r = nt(jnp.concatenate(rows, axis=0), s[b])
            field[b] = lanes_of(eighths(r), octet_key)
            return 0

        lax.fori_loop(first_group, first_group + count, step, 0, unroll=count)

    def uniform(lev):
        return lambda b, u: (8 * b + u, lev)

    def mixed(b, u):
        node = min(120 + u, 126)
        return node, max(k for k in range(7) if firsts[k] <= node)

    couple(0, 8, uniform(0))
    couple(8, 4, uniform(1))
    couple(12, 2, uniform(2))
    couple(14, 1, uniform(3))
    couple(15, 1, mixed)

    for k in range(1, 8):
        source = (z + 8 - k) % 8
        remote(
            topz.at[z], topz.at[source], b_send.at[k], b_recv.at[source], b_peer(k)
        ).wait_recv()
    pairs = [jnp.concatenate([topz[2 * h], topz[2 * h + 1]], axis=1) for h in range(4)]
    ordered = nn(jnp.concatenate(pairs, axis=0), perm[...]).astype(BF16)
    for b in range(4):
        topc[b] = ordered[16 * b : 16 * b + 16]
    for b in range(3):
        topc[4 + b] = up(topc[2 * b], topc[2 * b + 1], wtop[b])
    last = jnp.zeros((16, 256), BF16)
    for _ in range(3):
        last = up(topc[6], last, wtop[3])
    topc[7] = last
    r = nn(topc[...].reshape(128, 256), rep[...]).astype(BF16)
    for b in range(8):
        for m in range(8):
            tope[8 * b + m] = r[16 * b : 16 * b + 16, 128 * m : 128 * m + 128]

    sources = []
    for height in range(1, 7):
        node = 64 - (128 >> height) + me // (1 << height)
        parts = []
        for f in range(6):
            g = top_far[f, node] & ((64 >> height) - 1)
            if height == 1:
                place = (g & 7) * 4 + (g >> 3)
            elif height == 2:
                place = 32 + (g & 3) * 4 + (g >> 2)
            elif height == 3:
                place = 48 + (g & 1) * 4 + (g >> 1)
            else:
                place = 64 - (128 >> height) + g
            parts.append(tope[place])
        sources.append(gathered(parts))
    r = nt(jnp.concatenate(sources, axis=0), stop[...].reshape(192, 256))
    fields = r[80:96]
    key = iota((16, 192), 1) >> 5
    for h in range(5):
        fields = jnp.where(key == h, r[16 * h : 16 * h + 16], fields)
    from_above = nn(fields.astype(BF16), above_path[...].reshape(192, 256))

    def down(x, mat):
        lower = jnp.where(low, x, 0.0).astype(BF16)
        upper = jnp.where(low, 0.0, x).astype(BF16)
        r = nn(jnp.concatenate([lower, upper], axis=0), mat)
        return r[:16], r[16:]

    base = jnp.where(octet_key == 7, 0.0, field[15]) + from_above
    here = base
    for _ in range(2):
        here = base + down(here, w[7])[1]
    field[14] = field[14] + down(here, w[7])[0]
    for b in range(6, -1, -1):
        r0, r1 = down(field[8 + b], w[b])
        field[2 * b] = field[2 * b] + r0
        field[2 * b + 1] = field[2 * b + 1] + r1
    ordered = nt(field[0:8].reshape(128, 256).astype(BF16), perm[...])

    for b in range(8):
        x = ordered[16 * b : 16 * b + 16]
        rows = [jnp.where(group_key == m, x, 0.0).astype(BF16) for m in range(8)]
        r = nn(jnp.concatenate(rows, axis=0), basis[8 * b : 8 * b + 8].reshape(256, 128))
        for m in range(8):
            k = 8 * b + m
            out[:, 128 * k : 128 * k + 128] = (r[16 * m : 16 * m + 16] + acc[k]).astype(BF16)

    rhs_right.wait_send()
    rhs_left.wait_send()
    cf_right.wait_send()
    cf_left.wait_send()
    for copy in a_copies + b_copies:
        copy.wait_send()


def body(
    rhs_cols,
    near_blocks,
    near_list,
    leaf_basis,
    inner_transfer,
    inner_coupling,
    inner_far,
    top_transfer,
    top_coupling,
    top_far,
):
    hbm = pl.BlockSpec(memory_space=pl.ANY)
    vmem = pltpu.VMEM
    dma = pltpu.SemaphoreType.DMA
    return pl.pallas_call(
        kernel,
        out_shape=pltpu.VMEM((16, 8192), BF16),
        in_specs=[hbm] * 10,
        out_specs=pl.BlockSpec(memory_space=vmem),
        scratch_shapes=[
            vmem((16, 8192), BF16),
            pltpu.SMEM((4, 64), I32),
            pltpu.SMEM((6, 127), I32),
            pltpu.SMEM((6, 63), I32),
            vmem((64, 4, 128, 128), BF16),
            vmem((64, 32, 128), BF16),
            vmem((32, 32, 127), BF16),
            vmem((6, 32, 32, 127), BF16),
            vmem((32, 32, 62), BF16),
            vmem((6, 32, 32, 63), BF16),
            vmem((32, 32, 128), F32),
            vmem((32, 32, 128), F32),
            vmem((256, 16, 128), BF16),
            vmem((64, 16, 128), F32),
            vmem((8, 256, 256), BF16),
            vmem((4, 256, 256), BF16),
            vmem((128, 256), BF16),
            vmem((16, 256, 256), BF16),
            vmem((6, 32, 256), BF16),
            vmem((6, 32, 256), BF16),
            vmem((256, 256), BF16),
            vmem((256, 1024), BF16),
            vmem((3, 16, 16, 256), BF16),
            vmem((512, 16, 128), BF16),
            vmem((16, 16, 256), F32),
            vmem((8, 16, 128), BF16),
            vmem((8, 16, 128), BF16),
            vmem((8, 16, 256), BF16),
            vmem((64, 16, 128), BF16),
            dma((9 + CHUNKS,)),
            dma((2,)),
            dma((2,)),
            dma((2,)),
            dma((2,)),
            dma((8,)),
            dma((8,)),
            dma((8,)),
            dma((8,)),
        ],
        compiler_params=pltpu.CompilerParams(
            collective_id=0, has_side_effects=True, vmem_limit_bytes=56 * 1024 * 1024
        ),
        name="h2_product",
    )(
        near_list.T,
        inner_far.T,
        top_far.T,
        rhs_cols,
        near_blocks,
        leaf_basis,
        inner_transfer.transpose(1, 2, 0),
        inner_coupling.transpose(1, 2, 3, 0),
        top_transfer.transpose(1, 2, 0),
        top_coupling.transpose(1, 2, 3, 0),
    )


def solution(mesh):
    return jax.shard_map(
        body,
        mesh=mesh,
        in_specs=(
            P("rhs", "leaf"),
            P("leaf", None, None, None),
            P("leaf", None),
            P("leaf", None, None),
            P("leaf", None, None),
            P("leaf", None, None, None),
            P("leaf", None),
            P(),
            P(),
            P(),
        ),
        out_specs=P("rhs", "leaf"),
        check_vma=False,
    )
```

```python
import functools

import jax
import jax.numpy as jnp
from jax import lax
from jax.experimental import pallas as pl
from jax.experimental.pallas import tpu as pltpu
from jax.sharding import PartitionSpec as P

MESH = pl.DeviceIdType.MESH
F32 = jnp.float32
BF16 = jnp.bfloat16
I32 = jnp.int32
CHUNKS = 2


def nt(a, b):
    return lax.dot_general(a, b, (((1,), (1,)), ((), ())), preferred_element_type=F32)


def nn(a, b):
    return lax.dot_general(a, b, (((1,), (0,)), ((), ())), preferred_element_type=F32)


def iota(shape, dim):
    return lax.broadcasted_iota(I32, shape, dim)


def ones_where(cond):
    return jnp.where(cond, 1.0, 0.0).astype(BF16)


def lanes_of(rows, key):
    out = rows[7]
    for m in range(7):
        out = jnp.where(key == m, rows[m], out)
    return out


def eighths(r):
    return [r[16 * m : 16 * m + 16] for m in range(8)]


def top_place(t):
    return jnp.where(
        t < 32,
        (t & 7) * 4 + (t >> 3),
        jnp.where(
            t < 48,
            32 + (t & 3) * 4 + ((t - 32) >> 2),
            jnp.where(t < 56, 48 + (t & 1) * 4 + ((t - 48) >> 1), t),
        ),
    )


def top_parent(place):
    return jnp.where(
        place < 56,
        32 + (place >> 3) * 4 + (place & 3),
        jnp.where(place < 60, 60 + ((place - 56) >> 1), 62),
    )


def kernel(
    near_list_in,
    inner_far_in,
    top_far_in,
    rhs,
    near,
    basis_in,
    tr_in,
    cp_in,
    ttr_in,
    tcp_in,
    out,
    rhs_v,
    near_list,
    inner_far,
    top_far,
    near_v,
    basis,
    tr,
    cp,
    ttr,
    tcp,
    trf,
    ttrf,
    ext,
    acc,
    w,
    wtop,
    wrep,
    s,
    stop,
    above_path,
    perm,
    rep,
    cfx,
    cfe,
    field,
    roots,
    topz,
    topc,
    tope,
    loc,
    rhs_send,
    rhs_recv,
    cf_send,
    cf_recv,
    a_send,
    a_recv,
    b_send,
    b_recv,
):
    me = lax.axis_index("leaf")
    col = lax.axis_index("rhs")
    core = me % 2
    z = (me // 2) % 8
    y = me // 16
    slot = y * 2 + core

    def local(src, dst, k):
        copy = pltpu.make_async_copy(src, dst, loc.at[k])
        copy.start()
        return copy

    rhs_copy = local(rhs, rhs_v, 0)
    basis_copy = local(basis_in, basis, 1)
    tr_copy = local(tr_in, tr, 2)
    ttr_copy = local(ttr_in, ttr, 3)
    cp_copy = local(cp_in, cp, 4)
    tcp_copy = local(tcp_in, tcp, 5)
    list_copies = [
        local(near_list_in, near_list, 6 + CHUNKS),
        local(inner_far_in, inner_far, 7 + CHUNKS),
        local(top_far_in, top_far, 8 + CHUNKS),
    ]
    per = 64 // CHUNKS
    near_copies = [
        local(near.at[pl.ds(per * k, per)], near_v.at[pl.ds(per * k, per)], 6 + k)
        for k in range(CHUNKS)
    ]

    right = (me + 1) % 64
    left = (me + 63) % 64

    def a_peer(k):
        other = (slot + k) % 8
        return ((other // 2) * 8 + z) * 2 + other % 2

    def b_peer(k):
        return (y * 8 + (z + k) % 8) * 2 + core

    barrier = pltpu.get_barrier_semaphore()
    for peer in [right, left] + [a_peer(k) for k in range(1, 8)] + [b_peer(k) for k in range(1, 8)]:
        pl.semaphore_signal(barrier, inc=1, device_id=(peer, col), device_id_type=MESH)

    row, lane = iota((256, 256), 0), iota((256, 256), 1)
    perm[...] = ones_where(((row >> 5) == (lane & 7)) & ((row & 31) == (lane >> 3)))
    lane = iota((16, 256), 1)
    octet_key = lane & 7
    group_key = lane >> 5

    own = (me % 4) * 64
    rhs_copy.wait()
    for k in range(64):
        ext[own + k] = rhs_v[:, 128 * k : 128 * k + 128]

    def remote(src, dst, send, recv, peer):
        return pltpu.make_async_remote_copy(
            src_ref=src,
            dst_ref=dst,
            send_sem=send,
            recv_sem=recv,
            device_id=(peer, col),
            device_id_type=MESH,
        )

    mine = ext.at[pl.ds(own, 64)]
    rhs_right = remote(mine, mine, rhs_send.at[0], rhs_recv.at[0], right)
    rhs_left = remote(mine, mine, rhs_send.at[1], rhs_recv.at[1], left)

    basis_copy.wait()

    def leaf_up(b, _):
        x = ext[pl.ds(own + 8 * b, 8)].reshape(128, 128)
        u = basis[pl.ds(8 * b, 8)].reshape(256, 128)
        cfx[1, b] = lanes_of(eighths(nt(x, u)), group_key).astype(BF16)
        return 0

    lax.fori_loop(0, 8, leaf_up, 0, unroll=8)
    ordered = nn(cfx[1, 0:8].reshape(128, 256), perm[...]).astype(BF16)
    for b in range(8):
        cfx[1, b] = ordered[16 * b : 16 * b + 16]

    tr_copy.wait()
    lane = iota((64, 128), 1)
    own_parent = ones_where((iota((64, 128), 0) == (lane >> 1)) & (lane < 127))
    lane = iota((8, 128), 1)
    own_mask = ones_where(iota((8, 128), 0) == (lane & 7)).astype(F32)
    trf[...] = jnp.zeros_like(trf)
    trf[:, :, 0:127] = tr[...].astype(F32)

    def spread(ref, i, mask):
        rows = [jnp.broadcast_to(ref[i, j : j + 1, :], (8, 128)) * mask for j in range(32)]
        return jnp.concatenate(rows, axis=0).astype(BF16)

    def put(dst, at, pair, count, start):
        for g in range(count):
            both = [r[start + 8 * g : start + 8 * g + 8] for r in pair]
            dst[g, at, :] = jnp.concatenate(both, axis=0).astype(BF16)

    def transfer_rows(q, _):
        at = pl.ds(pl.multiple_of(16 * q, 16), 16)
        put(w, at, [nt(own_parent, spread(trf, 2 * q + e, own_mask)) for e in range(2)], 8, 0)
        return 0

    lax.fori_loop(0, 16, transfer_rows, 0, unroll=16)
    row, lane = iota((128, 256), 0), iota((128, 256), 1)
    root_rows = ones_where((lane & 7 == 7) & ((lane >> 3) == (row & 31)))
    wrep[...] = nn(root_rows, w[7]).astype(BF16)

    low = octet_key < 4

    def up(x0, x1, mat):
        r = nt(jnp.concatenate([x0, x1], axis=0), mat)
        return jnp.where(low, r[:16], r[16:]).astype(BF16)

    for b in range(7):
        cfx[1, 8 + b] = up(cfx[1, 2 * b], cfx[1, 2 * b + 1], w[b])
    last = jnp.zeros((16, 256), BF16)
    for _ in range(3):
        last = up(cfx[1, 14], last, w[7])
    cfx[1, 15] = last
    roots[slot] = nt(last, wrep[...]).astype(BF16)

    a_copies = [
        remote(roots.at[slot], roots.at[slot], a_send.at[k], a_recv.at[slot], a_peer(k))
        for k in range(1, 8)
    ]
    pl.semaphore_wait(barrier, 16)
    for copy in a_copies:
        copy.start()
    cf_right = remote(cfx.at[1], cfx.at[0], cf_send.at[0], cf_recv.at[0], right)
    cf_left = remote(cfx.at[1], cfx.at[2], cf_send.at[1], cf_recv.at[1], left)
    cf_right.start()
    cf_left.start()
    rhs_right.start()
    rhs_left.start()

    row, lane = iota((256, 1024), 0), iota((256, 1024), 1)
    rep[...] = ones_where(((row >> 3) == (lane & 31)) & ((row & 7) == (lane >> 7)))

    cp_copy.wait()
    tcp_copy.wait()
    ttr_copy.wait()
    ttrf[...] = jnp.zeros_like(ttrf)
    ttrf[:, :, 0:62] = ttr[...].astype(F32)
    top_mask = ones_where(iota((8, 128), 0) == (top_place(iota((8, 128), 1)) & 7)).astype(F32)
    lane = iota((32, 128), 1)
    top_picks = ones_where((lane < 62) & (iota((32, 128), 0) + 32 == top_parent(top_place(lane))))

    def coupling_rows(q, _):
        at = pl.ds(pl.multiple_of(16 * q, 16), 16)
        pair = []
        for e in range(2):
            rows = [cp[f, 2 * q + e] for f in range(6)]
            turned = jnp.transpose(jnp.concatenate(rows, axis=0).astype(F32))
            turned = jnp.concatenate([turned, jnp.zeros((1, 192), F32)], axis=0)
            pair.append(jnp.concatenate([turned, jnp.zeros((128, 64), F32)], axis=1))
        put(s, at, pair, 16, 0)
        put(wtop, at, [nt(top_picks, spread(ttrf, 2 * q + e, top_mask)) for e in range(2)], 4, 0)
        return 0

    lax.fori_loop(0, 16, coupling_rows, 0, unroll=16)

    level = (iota((48, 63), 0) >> 3) + 1
    mine = 64 - (128 >> level) + (me >> level) == iota((48, 63), 1)
    chosen = [ones_where(mine & ((iota((48, 63), 0) & 7) == e)) for e in range(8)]
    blank = jnp.zeros((32, 63), BF16)
    eights = []
    for o in range(4):
        total = None
        for e in range(8):
            i = 8 * o + e
            rows = [tcp[f, i] for f in range(6)] + [ttrf[i, :, 0:63].astype(BF16), blank]
            r = nt(chosen[e], jnp.concatenate(rows, axis=0))
            total = r if total is None else total + r
        eights.append(total)
    for h in range(6):
        stop[h] = jnp.concatenate([r[8 * h : 8 * h + 8] for r in eights], axis=0).astype(BF16)
    path = wrep[0:32, :]
    above_path[0] = path
    for h in range(5):
        padded = jnp.concatenate([jnp.zeros((64, 256), BF16), path, jnp.zeros((32, 256), BF16)], axis=0)
        path = nn(stop[h, :, 128:256], padded).astype(BF16)
        above_path[h + 1] = path

    group = group_key[:, :128]
    nought = jnp.zeros((16, 128), BF16)

    def gathered(parts):
        lo = parts[3]
        for m in (2, 1, 0):
            lo = jnp.where(group == m, parts[m], lo)
        hi = jnp.where(group == 0, parts[4], jnp.where(group == 1, parts[5], nought))
        return jnp.concatenate([lo, hi], axis=1)

    for copy in list_copies:
        copy.wait()

    cf_right.wait_recv()
    cf_left.wait_recv()
    firsts = [0, 64, 96, 112, 120, 124, 126]
    for side in range(3):
        for h in range(2):
            r = nn(cfx[side, 8 * h : 8 * h + 8].reshape(128, 256), rep[...]).astype(BF16)
            for u in range(8):
                for m in range(8):
                    node = 64 * h + 8 * u + m
                    if node == 127:
                        continue
                    lev = max(k for k in range(7) if firsts[k] <= node)
                    place = 4 * firsts[lev] + (me + side + 3) % 4 * (64 >> lev) + node - firsts[lev]
                    cfe[place] = r[16 * u : 16 * u + 16, 128 * m : 128 * m + 128]

    def couple(first_group, count, nodes_of):
        def step(b, _):
            rows = []
            for u in range(8):
                node, lev = nodes_of(b, u)
                ring = (256 >> lev) - 1
                rows.append(
                    gathered(
                        [cfe[4 * firsts[lev] + (inner_far[f, node] & ring)] for f in range(6)]
                    )
                )
            r = nt(jnp.concatenate(rows, axis=0), s[b])
            field[b] = lanes_of(eighths(r), octet_key)
            return 0

        lax.fori_loop(first_group, first_group + count, step, 0, unroll=count)

    def uniform(lev):
        return lambda b, u: (8 * b + u, lev)

    def mixed(b, u):
        node = min(120 + u, 126)
        return node, max(k for k in range(7) if firsts[k] <= node)

    couple(0, 8, uniform(0))
    couple(8, 4, uniform(1))
    couple(12, 2, uniform(2))
    couple(14, 1, uniform(3))
    couple(15, 1, mixed)

    rhs_right.wait_recv()
    rhs_left.wait_recv()

    def near_leaf(k, _):
        part = [ext[near_list[f, k] & 255] for f in range(4)]
        total = None
        for h in range(2):
            x = jnp.concatenate([part[2 * h], part[2 * h + 1]], axis=1)
            v = jnp.concatenate([near_v[k, 2 * h], near_v[k, 2 * h + 1]], axis=1)
            r = nt(x, v)
            total = r if total is None else total + r
        acc[k] = total
        return 0

    for k in range(1, 8):
        source = (slot + 8 - k) % 8
        remote(
            roots.at[slot], roots.at[source], a_send.at[k], a_recv.at[source], a_peer(k)
        ).wait_recv()
    packed = None
    for m in (3, 2, 1, 0):
        pair = roots[2 * m].astype(F32) + roots[2 * m + 1].astype(F32)
        packed = pair if packed is None else jnp.where(group_key[:, :128] == m, pair, packed)
    topz[z] = packed.astype(BF16)
    b_copies = [
        remote(topz.at[z], topz.at[z], b_send.at[k], b_recv.at[z], b_peer(k)) for k in range(1, 8)
    ]
    for copy in b_copies:
        copy.start()

    for k in range(0, 2):
        near_copies[k].wait()
        lax.fori_loop(per * k, per * k + per, near_leaf, 0, unroll=32)

    for k in range(1, 8):
        source = (z + 8 - k) % 8
        remote(
            topz.at[z], topz.at[source], b_send.at[k], b_recv.at[source], b_peer(k)
        ).wait_recv()
    pairs = [jnp.concatenate([topz[2 * h], topz[2 * h + 1]], axis=1) for h in range(4)]
    ordered = nn(jnp.concatenate(pairs, axis=0), perm[...]).astype(BF16)
    for b in range(4):
        topc[b] = ordered[16 * b : 16 * b + 16]
    for b in range(3):
        topc[4 + b] = up(topc[2 * b], topc[2 * b + 1], wtop[b])
    last = jnp.zeros((16, 256), BF16)
    for _ in range(3):
        last = up(topc[6], last, wtop[3])
    topc[7] = last
    r = nn(topc[...].reshape(128, 256), rep[...]).astype(BF16)
    for b in range(8):
        for m in range(8):
            tope[8 * b + m] = r[16 * b : 16 * b + 16, 128 * m : 128 * m + 128]

    sources = []
    for height in range(1, 7):
        node = 64 - (128 >> height) + me // (1 << height)
        parts = []
        for f in range(6):
            g = top_far[f, node] & ((64 >> height) - 1)
            if height == 1:
                place = (g & 7) * 4 + (g >> 3)
            elif height == 2:
                place = 32 + (g & 3) * 4 + (g >> 2)
            elif height == 3:
                place = 48 + (g & 1) * 4 + (g >> 1)
            else:
                place = 64 - (128 >> height) + g
            parts.append(tope[place])
        sources.append(gathered(parts))
    r = nt(jnp.concatenate(sources, axis=0), stop[...].reshape(192, 256))
    fields = r[80:96]
    key = iota((16, 192), 1) >> 5
    for h in range(5):
        fields = jnp.where(key == h, r[16 * h : 16 * h + 16], fields)
    from_above = nn(fields.astype(BF16), above_path[...].reshape(192, 256))

    def down(x, mat):
        lower = jnp.where(low, x, 0.0).astype(BF16)
        upper = jnp.where(low, 0.0, x).astype(BF16)
        r = nn(jnp.concatenate([lower, upper], axis=0), mat)
        return r[:16], r[16:]

    base = jnp.where(octet_key == 7, 0.0, field[15]) + from_above
    here = base
    for _ in range(2):
        here = base + down(here, w[7])[1]
    field[14] = field[14] + down(here, w[7])[0]
    for b in range(6, -1, -1):
        r0, r1 = down(field[8 + b], w[b])
        field[2 * b] = field[2 * b] + r0
        field[2 * b + 1] = field[2 * b + 1] + r1
    ordered = nt(field[0:8].reshape(128, 256).astype(BF16), perm[...])

    for b in range(8):
        x = ordered[16 * b : 16 * b + 16]
        rows = [jnp.where(group_key == m, x, 0.0).astype(BF16) for m in range(8)]
        r = nn(jnp.concatenate(rows, axis=0), basis[8 * b : 8 * b + 8].reshape(256, 128))
        for m in range(8):
            k = 8 * b + m
            out[:, 128 * k : 128 * k + 128] = (r[16 * m : 16 * m + 16] + acc[k]).astype(BF16)

    rhs_right.wait_send()
    rhs_left.wait_send()
    cf_right.wait_send()
    cf_left.wait_send()
    for copy in a_copies + b_copies:
        copy.wait_send()


def body(
    rhs_cols,
    near_blocks,
    near_list,
    leaf_basis,
    inner_transfer,
    inner_coupling,
    inner_far,
    top_transfer,
    top_coupling,
    top_far,
):
    hbm = pl.BlockSpec(memory_space=pl.ANY)
    vmem = pltpu.VMEM
    dma = pltpu.SemaphoreType.DMA
    return pl.pallas_call(
        kernel,
        out_shape=pltpu.VMEM((16, 8192), BF16),
        in_specs=[hbm] * 10,
        out_specs=pl.BlockSpec(memory_space=vmem),
        scratch_shapes=[
            vmem((16, 8192), BF16),
            pltpu.SMEM((4, 64), I32),
            pltpu.SMEM((6, 127), I32),
            pltpu.SMEM((6, 63), I32),
            vmem((64, 4, 128, 128), BF16),
            vmem((64, 32, 128), BF16),
            vmem((32, 32, 127), BF16),
            vmem((6, 32, 32, 127), BF16),
            vmem((32, 32, 62), BF16),
            vmem((6, 32, 32, 63), BF16),
            vmem((32, 32, 128), F32),
            vmem((32, 32, 128), F32),
            vmem((256, 16, 128), BF16),
            vmem((64, 16, 128), F32),
            vmem((8, 256, 256), BF16),
            vmem((4, 256, 256), BF16),
            vmem((128, 256), BF16),
            vmem((16, 256, 256), BF16),
            vmem((6, 32, 256), BF16),
            vmem((6, 32, 256), BF16),
            vmem((256, 256), BF16),
            vmem((256, 1024), BF16),
            vmem((3, 16, 16, 256), BF16),
            vmem((512, 16, 128), BF16),
            vmem((16, 16, 256), F32),
            vmem((8, 16, 128), BF16),
            vmem((8, 16, 128), BF16),
            vmem((8, 16, 256), BF16),
            vmem((64, 16, 128), BF16),
            dma((9 + CHUNKS,)),
            dma((2,)),
            dma((2,)),
            dma((2,)),
            dma((2,)),
            dma((8,)),
            dma((8,)),
            dma((8,)),
            dma((8,)),
        ],
        compiler_params=pltpu.CompilerParams(
            collective_id=0, has_side_effects=True, vmem_limit_bytes=56 * 1024 * 1024
        ),
        name="h2_product",
    )(
        near_list.T,
        inner_far.T,
        top_far.T,
        rhs_cols,
        near_blocks,
        leaf_basis,
        inner_transfer.transpose(1, 2, 0),
        inner_coupling.transpose(1, 2, 3, 0),
        top_transfer.transpose(1, 2, 0),
        top_coupling.transpose(1, 2, 3, 0),
    )


def solution(mesh):
    return jax.shard_map(
        body,
        mesh=mesh,
        in_specs=(
            P("rhs", "leaf"),
            P("leaf", None, None, None),
            P("leaf", None),
            P("leaf", None, None),
            P("leaf", None, None),
            P("leaf", None, None, None),
            P("leaf", None),
            P(),
            P(),
            P(),
        ),
        out_specs=P("rhs", "leaf"),
        check_vma=False,
    )
```
